512 devices in a mesh: gx: 8 (over y, z_hi), gy: 8 (over x, core), gz: 8 (over z_lo).
Axes of the slice: x: 4, y: 4, z: 16 (z_hi: 2, z_lo: 8; z = z_hi * 8 + z_lo), core: 2. Of those that a mesh axis runs over, the one named last changes fastest.
Arguments:
- density: bfloat16 [32, 128, 1024], P('gx', 'gy', 'gz'), may hold values from -6 to 6
- first_kernel: bfloat16 [3, 3, 3, 16, 1], replicated, may hold values from -1.75 to 1.75
- first_bias: float32 [16], replicated, may hold values from -2.5 to 2.5
- second_kernel: bfloat16 [3, 3, 3, 16, 16], replicated, may hold values from -0.4375 to 0.4375
- second_bias: float32 [16], replicated, may hold values from -2.5 to 2.5
- coarse_kernel: bfloat16 [3, 3, 3, 32, 16], replicated, may hold values from -0.4375 to 0.4375
- coarse_bias: float32 [32], replicated, may hold values from -2.5 to 2.5
- deeper_kernel: bfloat16 [3, 3, 3, 32, 32], replicated, may hold values from -0.3125 to 0.3125
- deeper_bias: float32 [32], replicated, may hold values from -2.5 to 2.5
- upward_kernel: bfloat16 [2, 2, 2, 16, 32], replicated, may hold values from -1.5 to 1.5
- upward_bias: float32 [16], replicated, may hold values from -2.5 to 2.5
- joined_kernel: bfloat16 [3, 3, 3, 16, 32], replicated, may hold values from -0.3125 to 0.3125
- joined_bias: float32 [16], replicated, may hold values from -2.5 to 2.5
- final_kernel: bfloat16 [3, 3, 3, 16, 16], replicated, may hold values from -0.4375 to 0.4375
- final_bias: float32 [16], replicated, may hold values from -2.5 to 2.5
- output_weight: bfloat16 [16], replicated, may hold values from -2 to 2
Outputs:
- predicted: float32 [32, 128, 1024], P('gx', 'gy', 'gz')
The draws below stay inside these ranges and needn't reach their ends.
All inputs are finite; a program needn't handle non-finite values.
Results may differ from the reference program's by a relative error of at most 0.02.
Values may be sent and summed in bfloat16 or wider, within the bound.
No kernel may reach another device: no remote copies, remote signals or barrier semaphores. Data moves between devices by JAX's collectives and lax.ppermute only.
A program may use at most 128 MiB of HBM per device.

```python
import math
import jax
import jax.numpy as jnp
from jax import lax

C0 = 16
C1 = 32
NX = 32
NY = 128
NZ = 1024


def block_levels(rng, shape, cuts, least, top_value):
    def one(dim, shards_of):
        steps = jax.random.uniform(jax.random.fold_in(jax.random.fold_in(rng, 6), dim), (shards_of,), jnp.float32, least / len(cuts), top_value / len(cuts))
        return jnp.repeat(jnp.exp(steps), shape[dim] // shards_of).reshape((-1,) + (1,) * (len(shape) - dim - 1))

    gain = one(*cuts[0])
    for cut in cuts[1:]:
        gain = gain * one(*cut)
    return gain


def normal_values(key, dims, scale, limit, cuts=(), kind=jnp.bfloat16):
    values = jax.random.normal(key, dims, jnp.float32) * scale
    if len(cuts) > 0:
        values = block_levels(key, dims, cuts, -0.22, 0.18) * values
    return jnp.clip(values, min=-limit, max=limit).astype(kind)


def setup_inputs(seed: int = 0) -> dict:
    key_list = jax.random.split(jax.random.key(seed), 17)
    density = normal_values(key_list[0], (NX, NY, NZ), 1.0, 6.0, ((0, 8), (1, 8), (2, 8)))
    first_kernel = normal_values(key_list[1], (3, 3, 3, C0, 1), 13 ** -0.5, 1.75)
    first_bias = normal_values(key_list[2], (C0,), 0.5, 2.5, (), jnp.float32)
    second_kernel = normal_values(key_list[3], (3, 3, 3, C0, C0), (27 * C0 // 2) ** -0.5, 0.4375)
    second_bias = normal_values(key_list[4], (C0,), 0.5, 2.5, (), jnp.float32)
    coarse_kernel = normal_values(key_list[5], (3, 3, 3, C1, C0), (27 * C0 // 2) ** -0.5, 0.4375)
    coarse_bias = normal_values(key_list[6], (C1,), 0.5, 2.5, (), jnp.float32)
    deeper_kernel = normal_values(key_list[7], (3, 3, 3, C1, C1), (27 * C1 // 2) ** -0.5, 0.3125)
    deeper_bias = normal_values(key_list[8], (C1,), 0.5, 2.5, (), jnp.float32)
    upward_kernel = normal_values(key_list[9], (2, 2, 2, C0, C1), (C1 // 2) ** -0.5, 1.5)
    upward_bias = normal_values(key_list[10], (C0,), 0.5, 2.5, (), jnp.float32)
    joined_kernel = normal_values(key_list[11], (3, 3, 3, C0, C1), (27 * C1 // 2) ** -0.5, 0.3125)
    joined_bias = normal_values(key_list[12], (C0,), 0.5, 2.5, (), jnp.float32)
    final_kernel = normal_values(key_list[13], (3, 3, 3, C0, C0), (27 * C0 // 2) ** -0.5, 0.4375)
    final_bias = normal_values(key_list[14], (C0,), 0.5, 2.5, (), jnp.float32)
    output_weight = normal_values(key_list[15], (C0,), (C0 // 2) ** -0.5, 2.0)
    return {"density": density, "first_kernel": first_kernel, "first_bias": first_bias, "second_kernel": second_kernel, "second_bias": second_bias, "coarse_kernel": coarse_kernel, "coarse_bias": coarse_bias, "deeper_kernel": deeper_kernel, "deeper_bias": deeper_bias, "upward_kernel": upward_kernel, "upward_bias": upward_bias, "joined_kernel": joined_kernel, "joined_bias": joined_bias, "final_kernel": final_kernel, "final_bias": final_bias, "output_weight": output_weight}


negative_slope = 0.2


def leaky_relu(values):
    return jnp.where(values > 0, values, negative_slope * values)


def convolve(volume, kernel, biases):
    channels, extent_x, extent_y, extent_z = volume.shape
    outputs = kernel.shape[3]
    slab_rows = math.gcd(extent_x, 8)
    padded = jnp.pad(volume, ((0, 0), (1, 1), (1, 1), (1, 1)), mode="wrap")
    starts = jnp.arange(extent_x // slab_rows, dtype=jnp.int32) * slab_rows
    kernel_wide = kernel.astype(jnp.float32)

    def one_slab(slab_start):
        window = lax.dynamic_slice_in_dim(padded, slab_start, slab_rows + 2, 1).astype(jnp.float32)
        summed = jnp.zeros((outputs, slab_rows, extent_y, extent_z), jnp.float32)
        for step_x in range(3):
            for step_y in range(3):
                for step_z in range(3):
                    shifted = window[:, step_x:step_x + slab_rows, step_y:step_y + extent_y, step_z:step_z + extent_z]
                    summed = summed + jnp.einsum("oi,ixyz->oxyz", kernel_wide[step_x, step_y, step_z], shifted)
        return leaky_relu(summed + biases[:, None, None, None]).astype(jnp.bfloat16)

    pieces = lax.map(one_slab, starts)
    return jnp.moveaxis(pieces, 0, 1).reshape(outputs, extent_x, extent_y, extent_z)


def pool_max(volume):
    channels, extent_x, extent_y, extent_z = volume.shape
    grouped = volume.reshape(channels, extent_x // 2, 2, extent_y // 2, 2, extent_z // 2, 2)
    return jnp.max(grouped, axis=(2, 4, 6))


def upsample(coarse_field, kernel, biases):
    channels, extent_x, extent_y, extent_z = coarse_field.shape
    outputs = kernel.shape[3]
    slab_rows = math.gcd(extent_x, 8)
    starts = jnp.arange(extent_x // slab_rows, dtype=jnp.int32) * slab_rows
    kernel_wide = kernel.astype(jnp.float32)

    def one_slab(slab_start):
        window = lax.dynamic_slice_in_dim(coarse_field, slab_start, slab_rows, 1).astype(jnp.float32)
        fine_cells = jnp.einsum("abcoi,ixyz->oxaybzc", kernel_wide, window)
        fine_cells = fine_cells.reshape(outputs, 2 * slab_rows, 2 * extent_y, 2 * extent_z)
        return leaky_relu(fine_cells + biases[:, None, None, None]).astype(jnp.bfloat16)

    pieces = lax.map(one_slab, starts)
    return jnp.moveaxis(pieces, 0, 1).reshape(outputs, 2 * extent_x, 2 * extent_y, 2 * extent_z)


def reference(density, first_kernel, first_bias, second_kernel, second_bias, coarse_kernel, coarse_bias, deeper_kernel, deeper_bias, upward_kernel, upward_bias, joined_kernel, joined_bias, final_kernel, final_bias, output_weight):
    first_field = convolve(density[None], first_kernel, first_bias)
    skipped = convolve(first_field, second_kernel, second_bias)
    pooled = pool_max(skipped)
    coarse_field = convolve(pooled, coarse_kernel, coarse_bias)
    deeper = convolve(coarse_field, deeper_kernel, deeper_bias)
    raised = upsample(deeper, upward_kernel, upward_bias)
    joined = jnp.concatenate([raised, skipped], axis=0)
    merged = convolve(joined, joined_kernel, joined_bias)
    final_field = convolve(merged, final_kernel, final_bias)
    flat = final_field.reshape(final_field.shape[0], -1)
    predicted = jnp.dot(output_weight[None, :], flat, preferred_element_type=jnp.float32)
    return predicted.reshape(final_field.shape[1:])
```

```python
import functools

import jax
import jax.numpy as jnp
from jax import lax
from jax.experimental import pallas as pl
from jax.experimental.pallas import tpu as pltpu
from jax.sharding import PartitionSpec as P

F32 = jnp.float32
BF16 = jnp.bfloat16
ROW = 72
WIDTH = 16 * ROW
INNER = slice(128, 1024)


def leaky(values):
    return jnp.maximum(values, 0.2 * values)


def iota(shape, dim):
    return lax.broadcasted_iota(jnp.int32, shape, dim)


def spread_bias(bias_ref, rows):
    count = bias_ref.shape[1]
    match = iota((rows, count), 0) % count == iota((rows, count), 1)
    return jnp.broadcast_to(jnp.sum(jnp.where(match, bias_ref[...], 0.0), axis=1, keepdims=True), (rows, 128))


def weights_kernel(half_ref, first_ref, second_ref, coarse_ref, deeper_ref, joined_ref, final_ref, upward_ref, output_ref,
                   b1_ref, b2_ref, b4_ref, b5_ref, b6_ref, b7_ref, b8_ref,
                   w1_ref, w2_ref, w4_ref, w5_ref, w7_ref, w8_ref, sz_ref, w6_ref, w9_ref, bias_ref,
                   fine_ref, joint_ref, coarse_base_ref, deeper_base_ref):
    tap = iota((27, 256), 0)
    lane = iota((27, 256), 1)
    place = (tap % 3) * 64 + (tap // 3 % 3) * 16 + tap // 9
    base = lax.dot_general(first_ref[...], (place == lane).astype(BF16), (((0,), (0,)), ((), ())),
                           preferred_element_type=F32)
    base = jnp.where(half_ref[0] == 0, base, pltpu.roll(base, 4, 1))
    old = iota((256, 256), 0)
    new = iota((256, 256), 1)
    order = (old % 16 // 8) * 128 + (old // 16 % 4) * 32 + (old // 64) * 8 + old % 8
    permute = (order == new).astype(BF16)
    for x in range(8):
        rows = jnp.concatenate(
            [pltpu.roll(base, x + 16 * b + 64 * e, 1) if x + b + e else base for b in range(2) for e in range(2)], axis=0)
        w1_ref[64 * x:64 * x + 64] = jnp.dot(rows.astype(BF16), permute, preferred_element_type=F32).astype(BF16)

    for source, target in ((second_ref, w2_ref), (final_ref, w8_ref)):
        fine_ref[...] = jnp.zeros_like(fine_ref)
        for t in range(27):
            at = (t // 3 % 3) * 64 + (t % 3) * 16
            fine_ref[16 * (t // 9):16 * (t // 9) + 16, at:at + 16] = source[16 * t:16 * t + 16].astype(F32)
        for u in range(3):
            block = fine_ref[16 * u:16 * u + 16]
            for n in range(4):
                move = (n // 2) * 64 + (n % 2) * 16
                at = 64 * u + 16 * n
                target[at:at + 16] = (pltpu.roll(block, move, 1) if n else block).astype(BF16)

    joint_ref[...] = jnp.zeros_like(joint_ref)
    for t in range(27):
        piece = joined_ref[16 * t:16 * t + 16].astype(F32)
        for side in range(2):
            at = side * 256 + (t // 3 % 3) * 64 + (t % 3) * 16
            joint_ref[16 * (t // 9):16 * (t // 9) + 16, at:at + 16] = piece[:, 16 * side:16 * side + 16]
    for u in range(3):
        block = joint_ref[16 * u:16 * u + 16]
        for n in range(4):
            move = (n // 2) * 64 + (n % 2) * 16
            at = 64 * u + 16 * n
            w7_ref[at:at + 16] = (pltpu.roll(block, move, 1) if n else block).astype(BF16)

    for source, scratch, target, width, count in (
        (coarse_ref, coarse_base_ref, w4_ref, 16, 3), (deeper_ref, deeper_base_ref, w5_ref, 32, 4)):
        scratch[...] = jnp.zeros_like(scratch)
        for t in range(27):
            scratch[:, width * t:width * t + width] = source[32 * t:32 * t + 32].astype(F32)
        block = scratch[...]
        for p in range(count):
            target[32 * p:32 * p + 32] = (pltpu.roll(block, 9 * width * p, 1) if p else block).astype(BF16)

    row = iota((256, 512), 0)
    col = iota((256, 512), 1)
    cell = jnp.where(row < 128, row + 8, jnp.where(row < 136, row - 128, row))
    sz_ref[...] = ((cell == 2 * (col % 128) + col // 128 - 1) & (row < 144)).astype(BF16)

    w6_ref[...] = upward_ref[...]
    spread = (iota((16, 64), 0) == iota((16, 64), 1) % 16).astype(BF16)
    row_weights = jnp.dot(output_ref[...], spread, preferred_element_type=F32)
    row = iota((8, 64), 0)
    group = iota((8, 64), 1) // 16
    chosen = (row % 2 == group // 2) & (row // 2 == group % 2)
    w9_ref[...] = jnp.where(chosen, row_weights, 0.0)
    for n, ref in enumerate((b1_ref, b2_ref, b6_ref, b7_ref, b8_ref, b4_ref, b5_ref)):
        bias_ref[n] = spread_bias(ref, 64)


def prepare_weights(half, *parameters):
    shapes = [(512, 256), (192, 256), (96, 768), (128, 1792), (192, 512), (192, 256), (256, 512), (128, 32)]
    vmem = pl.BlockSpec(memory_space=pltpu.VMEM)
    return pl.pallas_call(
        weights_kernel,
        out_shape=[jax.ShapeDtypeStruct(s, BF16) for s in shapes]
        + [jax.ShapeDtypeStruct((8, 64), F32), jax.ShapeDtypeStruct((7, 64, 128), F32)],
        in_specs=[pl.BlockSpec(memory_space=pltpu.SMEM)] + [vmem] * len(parameters),
        out_specs=[vmem] * 10,
        scratch_shapes=[pltpu.VMEM((48, 256), F32), pltpu.VMEM((48, 512), F32),
                        pltpu.VMEM((32, 768), F32), pltpu.VMEM((32, 1792), F32)],
        compiler_params=pltpu.CompilerParams(vmem_limit_bytes=24 * 2**20),
        cost_estimate=pl.CostEstimate(flops=10**7, bytes_accessed=2 * 10**6, transcendentals=0),
        name="weights",
    )(half, *parameters)


def collect(low_ref, a_ref, mid_ref, b_ref, high_ref, all_ref):
    for g, ref in enumerate((a_ref, mid_ref, b_ref)):
        for x in range(8):
            at = 32 * (8 * g + x)
            all_ref[at:at + 8] = low_ref[8 * g + x].astype(F32)
            all_ref[at + 8:at + 24] = ref[x].astype(F32)
            all_ref[at + 24:at + 32] = high_ref[8 * g + x].astype(F32)


def edges_kernel(odd_ref, low_ref, a_ref, mid_ref, b_ref, high_ref, edge_a_ref, edge_b_ref, all_ref):
    collect(low_ref, a_ref, mid_ref, b_ref, high_ref, all_ref)
    left = jnp.zeros((48, 128), F32)
    right = jnp.zeros((48, 128), F32)
    lane = iota((48, 128), 1)
    for k in range(16):
        rows = all_ref[48 * k:48 * k + 48]
        inside = (lane >= 8 * k) & (lane < 8 * k + 8)
        left = jnp.where(inside, pltpu.roll(rows, 8 * k, 1) if k else rows, left)
        right = jnp.where(inside, pltpu.roll(rows, (8 * k + 8) % 128, 1) if k < 15 else rows, right)
    odd = odd_ref[1] == 1
    edge_a_ref[...] = jnp.where(odd, right, left).astype(BF16)
    edge_b_ref[...] = jnp.where(odd, left, right).astype(BF16)


def pack_edges(odd, *pieces):
    vmem = pl.BlockSpec(memory_space=pltpu.VMEM)
    return pl.pallas_call(
        edges_kernel,
        out_shape=[jax.ShapeDtypeStruct((48, 128), BF16)] * 2,
        in_specs=[pl.BlockSpec(memory_space=pltpu.SMEM)] + [vmem] * 5,
        out_specs=[vmem] * 2,
        scratch_shapes=[pltpu.VMEM((768, 128), F32)],
        compiler_params=pltpu.CompilerParams(vmem_limit_bytes=8 * 2**20),
        name="edges",
    )(odd, *pieces)


def chunks(width):
    return [slice(at, min(at + 256, width)) for at in range(0, width, 256)]


def moved(values, step):
    return pltpu.roll(values, step % values.shape[1], 1)


def window(values):
    rows = []
    for b in range(2):
        even = values[32 * b:32 * b + 16]
        odd = values[32 * b + 16:32 * b + 32]
        rows.append(jnp.concatenate([moved(odd, 1), even, odd, moved(even, -1)], axis=0))
    return jnp.concatenate([moved(rows[1], ROW), rows[0], rows[1], moved(rows[0], -ROW)], axis=0)


def neighbours(values):
    rows = jnp.concatenate([moved(values, 1), values, moved(values, -1)], axis=0)
    return jnp.concatenate([moved(rows, ROW), rows, moved(rows, -ROW)], axis=0)


def two_planes(sums_a, sums_b, acc_ref, part):
    done_a = acc_ref[1, :, part] + sums_a[128:192]
    done_b = acc_ref[0, :, part] + sums_a[64:128] + sums_b[128:192]
    acc_ref[1, :, part] = sums_a[0:64] + sums_b[64:128]
    acc_ref[0, :, part] = sums_b[0:64]
    return done_a, done_b


def paired_dots(w_ref, ref_a, ref_b, width):
    whole = width // 256 * 256
    for at in range(0, whole, 256):
        part = slice(at, at + 256)
        yield part, [jnp.dot(w_ref[...], ref[:, part], preferred_element_type=F32) for ref in (ref_a, ref_b)]
    if whole < width:
        part = slice(whole, width)
        both = jnp.dot(w_ref[...], jnp.concatenate([ref_a[:, part], ref_b[:, part]], axis=1), preferred_element_type=F32)
        yield part, [both[:, 0:width - whole], both[:, width - whole:]]


def wide(bias, values):
    rows, columns = values.shape
    bias = jnp.concatenate([bias] * (columns // 128), axis=1) if columns > 128 else bias
    return jnp.concatenate([bias] * (rows // bias.shape[0]), axis=0) if rows > bias.shape[0] else bias


def network_kernel(odd_ref, low_ref, a_ref, mid_ref, b_ref, high_ref, edge_a_ref, edge_b_ref,
                   w1_ref, w2_ref, w4_ref, w5_ref, w7_ref, w8_ref, sz_ref, w6_ref, w9_ref, bias_ref,
                   out_ref,
                   cells_ref, rim_ref, sampled_ref, phase_ref, col0_ref, first_ref, slot_a_ref, slot_b_ref, acc_ref,
                   skip_ref, pool_ref, col4_ref, col5_ref, col7_ref, col8_ref, flat_ref, last_ref):
    collect(low_ref, a_ref, mid_ref, b_ref, high_ref, cells_ref)
    rim_ref[...] = jnp.zeros_like(rim_ref)
    edge_a = edge_a_ref[...].astype(F32)
    edge_b = edge_b_ref[...].astype(F32)
    odd = odd_ref[1] == 1
    left = jnp.where(odd, edge_b, edge_a)
    right = jnp.where(odd, edge_a, edge_b)
    for k in range(16):
        rim_ref[48 * k:48 * k + 48, 0:8] = left[:, 8 * k:8 * k + 8]
        rim_ref[48 * k:48 * k + 48, 8:16] = right[:, 8 * k:8 * k + 8]
    for at in range(0, 768, 256):
        rows = jnp.concatenate([cells_ref[at:at + 256], rim_ref[at:at + 256]], axis=1).astype(BF16)
        sampled = jnp.dot(rows, sz_ref[...], preferred_element_type=F32)
        for w in range(4):
            sampled_ref[w, at:at + 256] = sampled[:, 128 * w:128 * w + 128]

    order = (2 - 2 * odd_ref[0], 1, 2 * odd_ref[0])
    for y in range(32):
        for w in range(4):
            column_of_x = sampled_ref.at[w][pl.ds(y, 24, stride=32), :]
            for g in range(3):
                phase_ref[3 * (y % 2) + order[g], 8 * w:8 * w + 8, ROW * (y // 2):ROW * (y // 2) + ROW] = column_of_x[
                    8 * g:8 * g + 8, 0:ROW]
    for g in range(3):
        even = phase_ref[g].astype(BF16)
        odd = phase_ref[3 + g].astype(BF16)
        col0_ref[128 * g:128 * g + 128] = jnp.concatenate([moved(odd, ROW), even, odd, moved(even, -ROW)], axis=0)

    bias = bias_ref[0]
    w1_first_ref = w1_ref.at[0:128, 0:128]
    for part, sums in paired_dots(w1_ref, col0_ref.at[0:256], col0_ref.at[128:384], WIDTH):
        for g in range(2):
            values = leaky(sums[g] + wide(bias, sums[g])).astype(BF16)
            first_ref[8 * g:8 * g + 8, :, part] = values.reshape(8, 64, values.shape[1])
    for part in chunks(WIDTH):
        sums = jnp.dot(w1_first_ref[...], col0_ref[256:384, part], preferred_element_type=F32)
        values = leaky(sums + wide(bias, sums)).astype(BF16)
        first_ref[16:18, :, part] = values.reshape(2, 64, values.shape[1])

    bias_second = bias_ref[1]

    def gather_first(j, slot_ref):
        for a in range(2):
            slot_ref[a] = window(first_ref[2 * j + a])

    def skipped_planes(j, slot_ref):
        for part, sums in paired_dots(w2_ref, slot_ref.at[0], slot_ref.at[1], WIDTH):
            top = None
            for a, done in enumerate(two_planes(*sums, acc_ref, part)):
                values = leaky(done + wide(bias_second, done))
                skip_ref[j, 64 * a:64 * a + 64, part] = values.astype(BF16)
                highest = jnp.max(values.reshape(4, 16, values.shape[1]), axis=0)
                top = highest if top is None else jnp.maximum(top, highest)
            pool_ref[j, :, part] = top.astype(BF16)

    gather_first(0, slot_a_ref)

    def two_steps(t, carry):
        gather_first(2 * t + 1, slot_b_ref)
        skipped_planes(2 * t, slot_a_ref)
        gather_first(2 * t + 2, slot_a_ref)
        skipped_planes(2 * t + 1, slot_b_ref)
        return carry

    lax.fori_loop(0, 4, two_steps, 0)
    skipped_planes(8, slot_a_ref)

    for s in range(8):
        col4_ref[144 * s:144 * s + 144] = neighbours(pool_ref[s + 1])[:, INNER]
    col4_ref[1152:1200] = jnp.zeros((48, 896), BF16)
    for d in range(4):
        for a in range(2):
            col7_ref[2 * d + a, 256:512] = window(skip_ref[d + 3, 64 * a:64 * a + 64])[:, INNER]
    bias_coarse = bias_ref[5, 0:32]
    parts = [[], []]
    for _, sums in paired_dots(w4_ref, col4_ref.at[0:768], col4_ref.at[432:1200], 896):
        for m in range(2):
            parts[m].append(leaky(sums[m] + wide(bias_coarse, sums[m])).astype(BF16))
    for m in range(2):
        values = jnp.concatenate(parts[m], axis=1)
        for p in range(3):
            at = 288 * (3 * m + p)
            col5_ref[at:at + 288] = neighbours(values[32 * p:32 * p + 32])
    col5_ref[1728:1792] = jnp.zeros((64, 896), BF16)

    bias_deeper = bias_ref[6, 0:32]
    bias_raised = bias_ref[2]
    parts = []
    for part in chunks(896):
        sums = jnp.dot(w5_ref[...], col5_ref[:, part], preferred_element_type=F32)
        parts.append(leaky(sums + wide(bias_deeper, sums)).astype(BF16))
    deeper = jnp.concatenate(parts, axis=1)
    for d in range(4):
        parts = []
        for part in chunks(896):
            sums = jnp.dot(w6_ref[...], deeper[32 * d:32 * d + 32, part], preferred_element_type=F32)
            parts.append(leaky(sums + wide(bias_raised, sums)).astype(BF16))
        values = jnp.concatenate(parts, axis=1)
        for a in range(2):
            col7_ref[2 * d + a, 0:256] = window(values[64 * a:64 * a + 64])

    bias_joined = bias_ref[3]
    for j in range(4):
        done = [two_planes(*sums, acc_ref, part)
                for part, sums in paired_dots(w7_ref, col7_ref.at[2 * j], col7_ref.at[2 * j + 1], 896)]
        if j > 0:
            for a in range(2):
                values = jnp.concatenate([leaky(pair[a] + wide(bias_joined, pair[a])).astype(BF16) for pair in done], axis=1)
                col8_ref[2 * j + a - 2] = window(values)[:, 128:768]

    bias_final = bias_ref[4]
    output_matrix = w9_ref[...].astype(BF16)
    for j in range(3):
        for part, sums in paired_dots(w8_ref, col8_ref.at[2 * j], col8_ref.at[2 * j + 1], 640):
            done = two_planes(*sums, acc_ref, part)
            if j > 0:
                for a in range(2):
                    values = leaky(done[a] + wide(bias_final, done[a])).astype(BF16)
                    predicted = jnp.dot(output_matrix, values, preferred_element_type=F32)
                    to = 4 * (j - 1) + 2 * a
                    flat_ref[0, to:to + 2, part] = predicted[0:2]
                    flat_ref[1, to:to + 2, part] = predicted[2:4]

    for y in range(8):
        at = ROW * (y + 4) - 256 + 4
        last_ref[8 * y:8 * y + 8, 0:64] = flat_ref[0, :, at:at + 64]
        last_ref[8 * y:8 * y + 8, 64:128] = flat_ref[1, :, at:at + 64]
    old = iota((128, 128), 0)
    turns = (2 * (old % 64) + old // 64 == iota((128, 128), 1)).astype(F32)
    result = jnp.dot(last_ref[...], turns, preferred_element_type=F32, precision=lax.Precision.HIGHEST)
    for y in range(8):
        for x in range(4):
            at = 8 * y + 2 * x
            out_ref[x, 2 * y:2 * y + 2, :] = result[at:at + 2]


def network(odd, pieces, weights):
    vmem = pl.BlockSpec(memory_space=pltpu.VMEM)
    scratch = [
        ((768, 128), F32), ((768, 128), F32), ((4, 768, 128), F32), ((6, 32, WIDTH), F32),
        ((384, WIDTH), BF16), ((18, 64, WIDTH), BF16), ((2, 256, WIDTH), BF16), ((2, 256, WIDTH), BF16),
        ((2, 64, WIDTH), F32), ((9, 128, WIDTH), BF16), ((9, 16, WIDTH), BF16),
        ((1200, 896), BF16), ((1792, 896), BF16), ((8, 512, 896), BF16), ((6, 256, 640), BF16),
        ((2, 8, 640), F32), ((64, 128), F32),
    ]
    operands = (odd, *pieces, *weights)
    return pl.pallas_call(
        network_kernel,
        out_shape=jax.ShapeDtypeStruct((4, 16, 128), F32),
        in_specs=[pl.BlockSpec(memory_space=pltpu.SMEM)] + [vmem] * (len(operands) - 1),
        out_specs=vmem,
        scratch_shapes=[pltpu.VMEM(shape, kind) for shape, kind in scratch],
        compiler_params=pltpu.CompilerParams(vmem_limit_bytes=50 * 2**20),
        cost_estimate=pl.CostEstimate(flops=4 * 10**9, bytes_accessed=4 * 10**6, transcendentals=0),
        name="network",
    )(*operands)


def ring(size, step):
    return [(i, (i + step) % size) for i in range(size)]


def partner(i, size, first):
    return (i + 1 if (i % 2 == 1) == first else i - 1) % size


def swaps_y(first):
    return [(gx, 2 * partner(gx // 2, 4, first) + gx % 2) for gx in range(8)]


def swaps_z(first):
    pairs = []
    for gx in range(8):
        for gz in range(8):
            to = partner(gx % 2 * 8 + gz, 16, first)
            pairs.append((gx * 8 + gz, (gx // 2 * 2 + to // 8) * 8 + to % 8))
    return pairs


def exchange(density, half, odd, pack):
    other = lax.ppermute(density, "gx", [(i, i ^ 1) for i in range(8)])
    other = yield other
    mid = jnp.concatenate([jnp.where(half == 0, density, other), jnp.where(half == 0, other, density)], axis=0)
    a = lax.ppermute(mid, "gx", swaps_y(False))
    b = lax.ppermute(mid, "gx", swaps_y(True))
    high = jnp.concatenate([a[:, 8:], mid[:, 8:], b[:, 8:]], axis=0)
    low = jnp.concatenate([a[:, :8], mid[:, :8], b[:, :8]], axis=0)
    low, high = lax.ppermute(high, "gy", ring(8, 1)), lax.ppermute(low, "gy", ring(8, -1))
    pieces = (low, a, mid, b, high)
    edge_a, edge_b = pack(odd, *pieces)
    edge_a = lax.ppermute(edge_a, ("gx", "gz"), swaps_z(True))
    edge_b = lax.ppermute(edge_b, ("gx", "gz"), swaps_z(False))
    yield *pieces, edge_a, edge_b


def body(density, first_kernel, first_bias, second_kernel, second_bias, coarse_kernel, coarse_bias, deeper_kernel,
         deeper_bias, upward_kernel, upward_bias, joined_kernel, joined_bias, final_kernel, final_bias, output_weight):
    half = (lax.axis_index("gx") % 2).astype(jnp.int32)
    odd = jnp.stack([lax.axis_index("gx") // 2 % 2, lax.axis_index("gz") % 2]).astype(jnp.int32)
    steps = exchange(density, half, odd, pack_edges)
    other = next(steps)
    weights = prepare_weights(
        half.reshape(1), first_kernel.reshape(27, 16), second_kernel.reshape(432, 16),
        coarse_kernel.reshape(864, 16), deeper_kernel.reshape(864, 32), joined_kernel.reshape(432, 32),
        final_kernel.reshape(432, 16), upward_kernel.reshape(128, 32), output_weight.reshape(1, 16),
        *(b.reshape(1, -1) for b in (first_bias, second_bias, coarse_bias, deeper_bias, upward_bias, joined_bias,
                                     final_bias)))
    other, weights = lax.optimization_barrier((other, weights))
    pieces = steps.send(other)
    return network(odd, pieces, weights)


def solution(mesh):
    placed = (P("gx", "gy", "gz"),) + (P(),) * 15
    return jax.shard_map(body, mesh=mesh, in_specs=placed, out_specs=P("gx", "gy", "gz"), check_vma=False)
```

```python
import functools

import jax
import jax.numpy as jnp
from jax import lax
from jax.experimental import pallas as pl
from jax.experimental.pallas import tpu as pltpu
from jax.sharding import PartitionSpec as P

F32 = jnp.float32
BF16 = jnp.bfloat16
ROW = 72
FINE = 1152
COARSE, COARSE_WIDTH = 128, 896
RAISED, RAISED_WIDTH = 200, 768
FINAL, FINAL_WIDTH = 272, 640


def leaky(values):
    return jnp.maximum(values, 0.2 * values)


def iota(shape, dim):
    return lax.broadcasted_iota(jnp.int32, shape, dim)


def spread_bias(bias, rows):
    count = bias.shape[1]
    match = iota((rows, count), 0) % count == iota((rows, count), 1)
    return jnp.broadcast_to(jnp.sum(jnp.where(match, bias, 0.0), axis=1, keepdims=True), (rows, 128))


def weights_kernel(place_ref, first_ref, *refs):
    kernels_ref, vectors_ref = refs[:2]
    (w1_ref, w2_ref, w4_ref, w5_ref, w7_ref, w8_ref, sz_ref, w6_ref, w9_ref, bias_ref, expand_ref, flags_ref) = refs[2:14]
    fine_ref, joint_ref, deeper_base_ref = refs[14:]

    tap = iota((27, 256), 0)
    lane = iota((27, 256), 1)
    place = (tap % 3) * 64 + (tap // 3 % 3) * 16 + tap // 9
    base = lax.dot_general(first_ref[...], (place == lane).astype(BF16), (((0,), (0,)), ((), ())),
                           preferred_element_type=F32)
    base = jnp.where(place_ref[0] == 0, base, pltpu.roll(base, 4, 1))
    old = iota((256, 256), 0)
    new = iota((256, 256), 1)
    order = (old % 16 // 8) * 128 + (old // 16 % 4) * 32 + (old // 64) * 8 + old % 8
    permute = (order == new).astype(BF16)
    for x in range(8):
        rows = jnp.concatenate(
            [pltpu.roll(base, x + 16 * b + 64 * e, 1) if x + b + e else base for b in range(2) for e in range(2)], axis=0)
        w1_ref[64 * x:64 * x + 64] = jnp.dot(rows.astype(BF16), permute, preferred_element_type=F32).astype(BF16)

    row = iota((128, 256), 0)
    sz_ref[...] = (iota((128, 256), 1) == (row % 2) * 128 + row // 2 + 4).astype(BF16)
    row = iota((256, 2 * FINE), 0)
    cell = row % 8 + 136 * (row // 128)
    target = (cell % 2) * FINE + (row % 128 // 8) * ROW + cell // 2
    expand_ref[...] = (iota((256, 2 * FINE), 1) == target).astype(BF16)
    for n in range(2):
        flags_ref[n] = jnp.full((8, 128), place_ref[n + 1].astype(F32))

    for side, target in ((0, w2_ref), (1, w8_ref)):
        fine_ref[...] = jnp.zeros_like(fine_ref)
        for t in range(27):
            at = (t // 3 % 3) * 64 + (t % 3) * 16
            fine_ref[16 * (t // 9):16 * (t // 9) + 16, at:at + 16] = kernels_ref[
                16 * t:16 * t + 16, 16 * side:16 * side + 16].astype(F32)
        for u in range(3):
            block = fine_ref[16 * u:16 * u + 16]
            for n in range(4):
                move = (n // 2) * 64 + (n % 2) * 16
                at = 64 * u + 16 * n
                target[at:at + 16] = (pltpu.roll(block, move, 1) if n else block).astype(BF16)

    joint_ref[...] = jnp.zeros_like(joint_ref)
    for t in range(27):
        piece = kernels_ref[432 + 16 * t:448 + 16 * t].astype(F32)
        for side in range(2):
            at = side * 256 + (t // 3 % 3) * 64 + (t % 3) * 16
            joint_ref[16 * (t // 9):16 * (t // 9) + 16, at:at + 16] = piece[:, 16 * side:16 * side + 16]
    for u in range(3):
        block = joint_ref[16 * u:16 * u + 16]
        for n in range(4):
            move = (n // 2) * 64 + (n % 2) * 16
            at = 64 * u + 16 * n
            w7_ref[at:at + 16] = (pltpu.roll(block, move, 1) if n else block).astype(BF16)

    same = (iota((432, 768), 0) == iota((432, 768), 1)).astype(BF16)
    block = lax.dot_general(kernels_ref[864:1296], same, (((0,), (0,)), ((), ())), preferred_element_type=F32)
    for p in range(3):
        w4_ref[32 * p:32 * p + 32] = (pltpu.roll(block, 144 * p, 1) if p else block).astype(BF16)
    deeper_base_ref[...] = jnp.zeros_like(deeper_base_ref)
    for t in range(27):
        deeper_base_ref[:, 32 * t:32 * t + 32] = kernels_ref[1296 + 32 * t:1328 + 32 * t].astype(F32)
    block = deeper_base_ref[...]
    for p in range(4):
        w5_ref[32 * p:32 * p + 32] = (pltpu.roll(block, 288 * p, 1) if p else block).astype(BF16)

    w6_ref[...] = kernels_ref[2160:2288]
    spread = (iota((16, 64), 0) == iota((16, 64), 1) % 16).astype(BF16)
    row_weights = jnp.dot(vectors_ref[:, 144:160].astype(BF16), spread, preferred_element_type=F32)
    row = iota((8, 64), 0)
    group = iota((8, 64), 1) // 16
    chosen = (row % 2 == group // 2) & (row // 2 == group % 2)
    w9_ref[...] = jnp.where(chosen, row_weights, 0.0)
    for n in range(5):
        bias_ref[n] = spread_bias(vectors_ref[:, 16 * n:16 * n + 16], 64)
    for n in range(2):
        bias_ref[5 + n] = spread_bias(vectors_ref[:, 80 + 32 * n:112 + 32 * n], 64)


def prepare_weights(place, first, kernels, vectors):
    shapes = [(512, 256), (192, 256), (96, 768), (128, 1792), (192, 512), (192, 256), (128, 256), (128, 32)]
    vmem = pl.BlockSpec(memory_space=pltpu.VMEM)
    return pl.pallas_call(
        weights_kernel,
        out_shape=[jax.ShapeDtypeStruct(s, BF16) for s in shapes]
        + [jax.ShapeDtypeStruct((8, 64), F32), jax.ShapeDtypeStruct((7, 64, 128), F32),
           jax.ShapeDtypeStruct((256, 2 * FINE), BF16), jax.ShapeDtypeStruct((2, 8, 128), F32)],
        in_specs=[pl.BlockSpec(memory_space=pltpu.SMEM)] + [vmem] * 3,
        out_specs=[vmem] * 12,
        scratch_shapes=[pltpu.VMEM((48, 256), F32), pltpu.VMEM((48, 512), F32), pltpu.VMEM((32, 1792), F32)],
        compiler_params=pltpu.CompilerParams(vmem_limit_bytes=24 * 2**20),
        cost_estimate=pl.CostEstimate(flops=10**7, bytes_accessed=2 * 10**6, transcendentals=0),
        name="weights",
    )(place, first, kernels, vectors)


def pick(flag, yes, no):
    rows = yes.shape[0] // 8
    return jnp.where((jnp.concatenate([flag] * rows, axis=0) if rows > 1 else flag) > 0.5, yes, no)


def edges_kernel(flags_ref, low_ref, a_ref, mid_ref, b_ref, high_ref, left_ref, right_ref, cells_ref):
    odd_y = flags_ref[0]
    for x in range(8):
        planes = [
            jnp.concatenate([low_ref[8 * g + x], ref[x], high_ref[8 * g + x]], axis=0).astype(F32)
            for g, ref in enumerate((a_ref, mid_ref, b_ref))
        ]
        cells_ref[32 * x:32 * x + 32] = pick(odd_y, planes[0], planes[2])
        cells_ref[32 * (8 + x):32 * (8 + x) + 32] = planes[1]
        cells_ref[32 * (16 + x):32 * (16 + x) + 32] = pick(odd_y, planes[2], planes[0])
    left = [jnp.zeros((24, 128), F32)] * 2
    right = [jnp.zeros((24, 128), F32)] * 2
    lane = iota((24, 128), 1)
    for y in range(32):
        b, at = y % 2, 8 * (y // 2)
        rows = cells_ref[pl.ds(y, 24, stride=32), :]
        inside = (lane >= at) & (lane < at + 8)
        left[b] = jnp.where(inside, pltpu.roll(rows, at, 1) if at else rows, left[b])
        right[b] = jnp.where(inside, pltpu.roll(rows, (at + 8) % 128, 1) if at < 120 else rows, right[b])
    left_ref[...] = jnp.concatenate(left, axis=0).astype(BF16)
    right_ref[...] = jnp.concatenate(right, axis=0).astype(BF16)


def pack_edges(flags, *pieces):
    vmem = pl.BlockSpec(memory_space=pltpu.VMEM)
    return pl.pallas_call(
        edges_kernel,
        out_shape=[jax.ShapeDtypeStruct((48, 128), BF16)] * 2 + [jax.ShapeDtypeStruct((768, 128), F32)],
        in_specs=[vmem] * 6,
        out_specs=[vmem] * 3,
        compiler_params=pltpu.CompilerParams(vmem_limit_bytes=8 * 2**20),
        name="edges",
    )(flags, *pieces)


def sample_kernel(cells_ref, sz_ref, phase_ref, even_ref, odd_ref):
    for at in range(0, 768, 256):
        sampled = jnp.dot(cells_ref[at:at + 256].astype(BF16), sz_ref[...], preferred_element_type=F32)
        even_ref[at:at + 256] = sampled[:, 0:128]
        odd_ref[at:at + 256] = sampled[:, 128:256]
    for y in range(32):
        to = ROW * (y // 2)
        for e, ref in enumerate((even_ref, odd_ref)):
            phase_ref[2 * (y % 2) + e, :, to:to + ROW] = ref[pl.ds(y, 24, stride=32), :][:, 0:ROW]


def sample(cells, sz):
    vmem = pl.BlockSpec(memory_space=pltpu.VMEM)
    return pl.pallas_call(
        sample_kernel,
        out_shape=jax.ShapeDtypeStruct((4, 24, FINE), F32),
        in_specs=[vmem] * 2,
        out_specs=vmem,
        scratch_shapes=[pltpu.VMEM((768, 128), F32), pltpu.VMEM((768, 128), F32)],
        compiler_params=pltpu.CompilerParams(vmem_limit_bytes=8 * 2**20),
        cost_estimate=pl.CostEstimate(flops=10**8, bytes_accessed=10**6, transcendentals=0),
        name="sample",
    )(cells, sz)


def chunks(width):
    return [slice(at, min(at + 256, width)) for at in range(0, width, 256)]


def moved(values, step):
    return pltpu.roll(values, step % values.shape[1], 1) if step else values


def shifted(values, start, width):
    whole = start // 128 * 128
    if start >= 0 and whole + width + 128 <= values.shape[1]:
        values, start = values[:, whole:whole + width + 128], start - whole
    return moved(values, -start)[:, 0:width]


def window(values, start, width):
    rows = []
    for b in range(2):
        even = values[32 * b:32 * b + 16]
        odd = values[32 * b + 16:32 * b + 32]
        rows.append(jnp.concatenate([moved(odd, 1), even, odd, moved(even, -1)], axis=0))
    return jnp.concatenate([shifted(rows[1], start - ROW, width), shifted(rows[0], start, width),
                            shifted(rows[1], start, width), shifted(rows[0], start + ROW, width)], axis=0)


def neighbours(values, start, width):
    rows = jnp.concatenate([moved(values, 1), values, moved(values, -1)], axis=0)
    return jnp.concatenate([shifted(rows, start + ROW * step, width) for step in (-1, 0, 1)], axis=0)


def two_planes(sums_a, sums_b, acc_ref, part):
    done_a = acc_ref[1, :, part] + sums_a[128:192]
    done_b = acc_ref[0, :, part] + sums_a[64:128] + sums_b[128:192]
    acc_ref[1, :, part] = sums_a[0:64] + sums_b[64:128]
    acc_ref[0, :, part] = sums_b[0:64]
    return done_a, done_b


def paired_dots(w_ref, ref_a, ref_b, width):
    whole = width // 256 * 256
    for at in range(0, whole, 256):
        part = slice(at, at + 256)
        yield part, [jnp.dot(w_ref[...], ref[:, part], preferred_element_type=F32) for ref in (ref_a, ref_b)]
    if whole < width:
        part = slice(whole, width)
        both = jnp.dot(w_ref[...], jnp.concatenate([ref_a[:, part], ref_b[:, part]], axis=1), preferred_element_type=F32)
        yield part, [both[:, 0:width - whole], both[:, width - whole:]]


def wide(bias, values):
    rows, columns = values.shape
    bias = jnp.concatenate([bias] * (columns // 128), axis=1) if columns > 128 else bias
    return jnp.concatenate([bias] * (rows // bias.shape[0]), axis=0) if rows > bias.shape[0] else bias


def network_kernel(flags_ref, center_ref, edge_a_ref, edge_b_ref,
                   w1_ref, w2_ref, w4_ref, w5_ref, w7_ref, w8_ref, w6_ref, w9_ref, bias_ref, expand_ref,
                   out_ref,
                   col0_ref, first_ref, slot_a_ref, slot_b_ref, acc_ref,
                   skip_ref, pool_ref, col4_ref, col5_ref, col7_ref, col8_ref, flat_ref, last_ref):
    odd_z = flags_ref[1]
    edge_a = edge_a_ref[...].astype(F32)
    edge_b = edge_b_ref[...].astype(F32)
    edges = jnp.concatenate([pick(odd_z, edge_b, edge_a), pick(odd_z, edge_a, edge_b)], axis=1).astype(BF16)
    rows = []
    for b in range(2):
        even, odd = [
            center_ref[2 * b + e] + jnp.dot(edges[24 * b:24 * b + 24], expand_ref[:, FINE * e:FINE * e + FINE],
                                            preferred_element_type=F32)
            for e in range(2)
        ]
        rows.append([moved(odd, 1), even, odd, moved(even, -1)])
    for g in range(3):
        even, odd = [
            jnp.concatenate([part[8 * g:8 * g + 8] for part in rows[b]], axis=0).astype(BF16) for b in range(2)
        ]
        col0_ref[128 * g:128 * g + 128] = jnp.concatenate([moved(odd, ROW), even, odd, moved(even, -ROW)], axis=0)

    bias = bias_ref[0]
    w1_first_ref = w1_ref.at[0:128, 0:128]
    for part, sums in paired_dots(w1_ref, col0_ref.at[0:256], col0_ref.at[128:384], FINE):
        for g in range(2):
            values = leaky(sums[g] + wide(bias, sums[g])).astype(BF16)
            first_ref[8 * g:8 * g + 8, :, part] = values.reshape(8, 64, values.shape[1])
    for part in chunks(FINE):
        sums = jnp.dot(w1_first_ref[...], col0_ref[256:384, part], preferred_element_type=F32)
        values = leaky(sums + wide(bias, sums)).astype(BF16)
        first_ref[16:18, :, part] = values.reshape(2, 64, values.shape[1])

    bias_second = bias_ref[1]

    def gather_first(j, slot_ref):
        for a in range(2):
            slot_ref[a] = window(first_ref[2 * j + a], 0, FINE)

    def skipped_planes(j, slot_ref):
        for part, sums in paired_dots(w2_ref, slot_ref.at[0], slot_ref.at[1], FINE):
            top = None
            for a, done in enumerate(two_planes(*sums, acc_ref, part)):
                values = leaky(done + wide(bias_second, done))
                skip_ref[j, 64 * a:64 * a + 64, part] = values.astype(BF16)
                highest = jnp.max(values.reshape(4, 16, values.shape[1]), axis=0)
                top = highest if top is None else jnp.maximum(top, highest)
            pool_ref[j, :, part] = top.astype(BF16)

    gather_first(0, slot_a_ref)

    def two_steps(t, carry):
        gather_first(2 * t + 1, slot_b_ref)
        skipped_planes(2 * t, slot_a_ref)
        gather_first(2 * t + 2, slot_a_ref)
        skipped_planes(2 * t + 1, slot_b_ref)
        return carry

    lax.fori_loop(0, 4, two_steps, 0)
    skipped_planes(8, slot_a_ref)

    for s in range(8):
        col4_ref[144 * s:144 * s + 144] = neighbours(pool_ref[s + 1], COARSE, COARSE_WIDTH)
    col4_ref[1152:1200] = jnp.zeros((48, COARSE_WIDTH), BF16)
    for d in range(4):
        for a in range(2):
            col7_ref[2 * d + a, 256:512] = window(skip_ref[d + 3, 64 * a:64 * a + 64], RAISED, RAISED_WIDTH)
    bias_coarse = bias_ref[5, 0:32]
    parts = [[], []]
    for _, sums in paired_dots(w4_ref, col4_ref.at[0:768], col4_ref.at[432:1200], COARSE_WIDTH):
        for m in range(2):
            parts[m].append(leaky(sums[m] + wide(bias_coarse, sums[m])).astype(BF16))
    for m in range(2):
        values = jnp.concatenate(parts[m], axis=1)
        for p in range(3):
            at = 288 * (3 * m + p)
            col5_ref[at:at + 288] = neighbours(values[32 * p:32 * p + 32], RAISED - COARSE, RAISED_WIDTH)
    col5_ref[1728:1792] = jnp.zeros((64, RAISED_WIDTH), BF16)

    bias_deeper = bias_ref[6, 0:32]
    bias_raised = bias_ref[2]
    parts = []
    for part in chunks(RAISED_WIDTH):
        sums = jnp.dot(w5_ref[...], col5_ref[:, part], preferred_element_type=F32)
        parts.append(leaky(sums + wide(bias_deeper, sums)).astype(BF16))
    deeper = jnp.concatenate(parts, axis=1)
    for d in range(4):
        parts = []
        for part in chunks(RAISED_WIDTH):
            sums = jnp.dot(w6_ref[...], deeper[32 * d:32 * d + 32, part], preferred_element_type=F32)
            parts.append(leaky(sums + wide(bias_raised, sums)).astype(BF16))
        values = jnp.concatenate(parts, axis=1)
        for a in range(2):
            col7_ref[2 * d + a, 0:256] = window(values[64 * a:64 * a + 64], 0, RAISED_WIDTH)

    bias_joined = bias_ref[3]
    for j in range(4):
        done = [two_planes(*sums, acc_ref, part)
                for part, sums in paired_dots(w7_ref, col7_ref.at[2 * j], col7_ref.at[2 * j + 1], RAISED_WIDTH)]
        if j > 0:
            for a in range(2):
                values = jnp.concatenate([leaky(pair[a] + wide(bias_joined, pair[a])).astype(BF16) for pair in done], axis=1)
                col8_ref[2 * j + a - 2] = window(values, FINAL - RAISED, FINAL_WIDTH)

    bias_final = bias_ref[4]
    output_matrix = w9_ref[...].astype(BF16)
    for j in range(3):
        for part, sums in paired_dots(w8_ref, col8_ref.at[2 * j], col8_ref.at[2 * j + 1], FINAL_WIDTH):
            done = two_planes(*sums, acc_ref, part)
            if j > 0:
                for a in range(2):
                    values = leaky(done[a] + wide(bias_final, done[a])).astype(BF16)
                    predicted = jnp.dot(output_matrix, values, preferred_element_type=F32)
                    to = 4 * (j - 1) + 2 * a
                    flat_ref[0, to:to + 2, part] = predicted[0:2]
                    flat_ref[1, to:to + 2, part] = predicted[2:4]

    for y in range(8):
        at = ROW * (y + 4) - FINAL + 4
        last_ref[8 * y:8 * y + 8, 0:64] = flat_ref[0, :, at:at + 64]
        last_ref[8 * y:8 * y + 8, 64:128] = flat_ref[1, :, at:at + 64]
    old = iota((128, 128), 0)
    turns = (2 * (old % 64) + old // 64 == iota((128, 128), 1)).astype(F32)
    result = jnp.dot(last_ref[...], turns, preferred_element_type=F32, precision=lax.Precision.HIGHEST)
    for y in range(8):
        for x in range(4):
            at = 8 * y + 2 * x
            out_ref[x, 2 * y:2 * y + 2, :] = result[at:at + 2]


def network(flags, center, edge_a, edge_b, weights):
    vmem = pl.BlockSpec(memory_space=pltpu.VMEM)
    scratch = [
        ((384, FINE), BF16), ((18, 64, FINE), BF16), ((2, 256, FINE), BF16), ((2, 256, FINE), BF16),
        ((2, 64, FINE), F32), ((9, 128, FINE), BF16), ((9, 16, FINE), BF16),
        ((1200, COARSE_WIDTH), BF16), ((1792, RAISED_WIDTH), BF16), ((8, 512, RAISED_WIDTH), BF16), ((6, 256, FINAL_WIDTH), BF16),
        ((2, 8, FINAL_WIDTH), F32), ((64, 128), F32),
    ]
    operands = (flags, center, edge_a, edge_b, *weights)
    return pl.pallas_call(
        network_kernel,
        out_shape=jax.ShapeDtypeStruct((4, 16, 128), F32),
        in_specs=[vmem] * len(operands),
        out_specs=vmem,
        scratch_shapes=[pltpu.VMEM(shape, kind) for shape, kind in scratch],
        compiler_params=pltpu.CompilerParams(vmem_limit_bytes=50 * 2**20),
        cost_estimate=pl.CostEstimate(flops=4 * 10**9, bytes_accessed=4 * 10**6, transcendentals=0),
        name="network",
    )(*operands)


def ring(size, step):
    return [(i, (i + step) % size) for i in range(size)]


def partner(i, size, first):
    return (i + 1 if (i % 2 == 1) == first else i - 1) % size


def swaps_y(first):
    return [(gx, 2 * partner(gx // 2, 4, first) + gx % 2) for gx in range(8)]


def swaps_z(first):
    pairs = []
    for gx in range(8):
        for gz in range(8):
            to = partner(gx % 2 * 8 + gz, 16, first)
            pairs.append((gx * 8 + gz, (gx // 2 * 2 + to // 8) * 8 + to % 8))
    return pairs


def exchange(density, half, pack):
    other = lax.ppermute(density, "gx", [(i, i ^ 1) for i in range(8)])
    other, flags = yield other
    mid = jnp.concatenate([jnp.where(half == 0, density, other), jnp.where(half == 0, other, density)], axis=0)
    a = lax.ppermute(mid, "gx", swaps_y(False))
    b = lax.ppermute(mid, "gx", swaps_y(True))
    high = jnp.concatenate([a[:, 8:], mid[:, 8:], b[:, 8:]], axis=0)
    low = jnp.concatenate([a[:, :8], mid[:, :8], b[:, :8]], axis=0)
    low, high = lax.ppermute(high, "gy", ring(8, 1)), lax.ppermute(low, "gy", ring(8, -1))
    left, right, cells = pack(flags, low, a, mid, b, high)
    odd = lax.axis_index("gz") % 2 == 1
    edge_a = lax.ppermute(jnp.where(odd, right, left), ("gx", "gz"), swaps_z(True))
    edge_b = lax.ppermute(jnp.where(odd, left, right), ("gx", "gz"), swaps_z(False))
    yield edge_a, edge_b, cells


def body(density, first_kernel, first_bias, second_kernel, second_bias, coarse_kernel, coarse_bias, deeper_kernel,
         deeper_bias, upward_kernel, upward_bias, joined_kernel, joined_bias, final_kernel, final_bias, output_weight):
    half = (lax.axis_index("gx") % 2).astype(jnp.int32)
    place = jnp.stack([half, lax.axis_index("gx") // 2 % 2, lax.axis_index("gz") % 2]).astype(jnp.int32)
    steps = exchange(density, half, pack_edges)
    other = next(steps)
    kernels = jnp.concatenate([
        jnp.concatenate([second_kernel, final_kernel], axis=4).reshape(432, 32), joined_kernel.reshape(432, 32),
        jnp.swapaxes(coarse_kernel, 3, 4).reshape(432, 32), deeper_kernel.reshape(864, 32), upward_kernel.reshape(128, 32),
    ], axis=0)
    vectors = jnp.concatenate([first_bias, second_bias, upward_bias, joined_bias, final_bias, coarse_bias, deeper_bias,
                               output_weight.astype(F32)]).reshape(1, 160)
    weights = prepare_weights(place, first_kernel.reshape(27, 16), kernels, vectors)
    other, weights = lax.optimization_barrier((other, weights))
    *weights, flags = weights
    sz = weights.pop(6)
    edge_a, edge_b, cells = steps.send((other, flags))
    return network(flags, sample(cells, sz), edge_a, edge_b, weights)


def solution(mesh):
    placed = (P("gx", "gy", "gz"),) + (P(),) * 15
    return jax.shard_map(body, mesh=mesh, in_specs=placed, out_specs=P("gx", "gy", "gz"), check_vma=False)
```

```python
import functools

import jax
import jax.numpy as jnp
from jax import lax
from jax.experimental import pallas as pl
from jax.experimental.pallas import tpu as pltpu
from jax.sharding import PartitionSpec as P

F32 = jnp.float32
BF16 = jnp.bfloat16
ROW = 72
FINE = 1152
COARSE, COARSE_WIDTH = 128, 896
RAISED, RAISED_WIDTH = 200, 768
FINAL, FINAL_WIDTH = 272, 640


def leaky(values):
    return jnp.maximum(values, 0.2 * values)


def iota(shape, dim):
    return lax.broadcasted_iota(jnp.int32, shape, dim)


def spread_bias(bias, rows):
    count = bias.shape[1]
    match = iota((rows, count), 0) % count == iota((rows, count), 1)
    return jnp.broadcast_to(jnp.sum(jnp.where(match, bias, 0.0), axis=1, keepdims=True), (rows, 128))


def weights_kernel(place_ref, first_ref, *refs):
    kernels_ref, vectors_ref = refs[:2]
    (w1_ref, w2_ref, w4_ref, w5_ref, w7_ref, w8_ref, sz_ref, w6_ref, w9_ref, bias_ref, expand_ref, flags_ref) = refs[2:14]
    fine_ref, joint_ref, deeper_base_ref = refs[14:]

    tap = iota((27, 256), 0)
    lane = iota((27, 256), 1)
    place = (tap % 3) * 64 + (tap // 3 % 3) * 16 + tap // 9
    base = lax.dot_general(first_ref[...], (place == lane).astype(BF16), (((0,), (0,)), ((), ())),
                           preferred_element_type=F32)
    base = jnp.where(place_ref[0] == 0, base, pltpu.roll(base, 4, 1))
    old = iota((256, 256), 0)
    new = iota((256, 256), 1)
    order = (old % 16 // 8) * 128 + (old // 16 % 4) * 32 + (old // 64) * 8 + old % 8
    permute = (order == new).astype(BF16)
    for x in range(8):
        rows = jnp.concatenate(
            [pltpu.roll(base, x + 16 * b + 64 * e, 1) if x + b + e else base for b in range(2) for e in range(2)], axis=0)
        w1_ref[64 * x:64 * x + 64] = jnp.dot(rows.astype(BF16), permute, preferred_element_type=F32).astype(BF16)

    row = iota((128, 256), 0)
    sz_ref[...] = (iota((128, 256), 1) == (row % 2) * 128 + row // 2 + 4).astype(BF16)
    row = iota((256, 2 * FINE), 0)
    cell = row % 8 + 136 * (row // 128)
    target = (cell % 2) * FINE + (row % 128 // 8) * ROW + cell // 2
    expand_ref[...] = (iota((256, 2 * FINE), 1) == target).astype(BF16)
    for n in range(2):
        flags_ref[n] = jnp.full((8, 128), place_ref[n + 1].astype(F32))

    for side, target in ((0, w2_ref), (1, w8_ref)):
        fine_ref[...] = jnp.zeros_like(fine_ref)
        for t in range(27):
            at = (t // 3 % 3) * 64 + (t % 3) * 16
            fine_ref[16 * (t // 9):16 * (t // 9) + 16, at:at + 16] = kernels_ref[
                16 * t:16 * t + 16, 16 * side:16 * side + 16].astype(F32)
        for u in range(3):
            block = fine_ref[16 * u:16 * u + 16]
            for n in range(4):
                move = (n // 2) * 64 + (n % 2) * 16
                at = 64 * u + 16 * n
                target[at:at + 16] = (pltpu.roll(block, move, 1) if n else block).astype(BF16)

    joint_ref[...] = jnp.zeros_like(joint_ref)
    for t in range(27):
        piece = kernels_ref[432 + 16 * t:448 + 16 * t].astype(F32)
        for side in range(2):
            at = side * 256 + (t // 3 % 3) * 64 + (t % 3) * 16
            joint_ref[16 * (t // 9):16 * (t // 9) + 16, at:at + 16] = piece[:, 16 * side:16 * side + 16]
    for u in range(3):
        block = joint_ref[16 * u:16 * u + 16]
        for n in range(4):
            move = (n // 2) * 64 + (n % 2) * 16
            at = 64 * u + 16 * n
            rows = (pltpu.roll(block, move, 1) if n else block).astype(BF16)
            for side in range(2):
                w7_ref[side, at:at + 16] = rows[:, 256 * side:256 * side + 256]

    same = (iota((432, 768), 0) == iota((432, 768), 1)).astype(BF16)
    block = lax.dot_general(kernels_ref[864:1296], same, (((0,), (0,)), ((), ())), preferred_element_type=F32)
    for p in range(3):
        w4_ref[32 * p:32 * p + 32] = (pltpu.roll(block, 144 * p, 1) if p else block).astype(BF16)
    deeper_base_ref[...] = jnp.zeros_like(deeper_base_ref)
    for t in range(27):
        deeper_base_ref[:, 32 * t:32 * t + 32] = kernels_ref[1296 + 32 * t:1328 + 32 * t].astype(F32)
    block = deeper_base_ref[...]
    for p in range(4):
        w5_ref[32 * p:32 * p + 32] = (pltpu.roll(block, 288 * p, 1) if p else block).astype(BF16)

    w6_ref[...] = kernels_ref[2160:2288]
    spread = (iota((16, 64), 0) == iota((16, 64), 1) % 16).astype(BF16)
    row_weights = jnp.dot(vectors_ref[:, 144:160].astype(BF16), spread, preferred_element_type=F32)
    row = iota((8, 64), 0)
    group = iota((8, 64), 1) // 16
    chosen = (row % 2 == group // 2) & (row // 2 == group % 2)
    w9_ref[...] = jnp.where(chosen, row_weights, 0.0)
    for n in range(5):
        bias_ref[n] = spread_bias(vectors_ref[:, 16 * n:16 * n + 16], 64)
    for n in range(2):
        bias_ref[5 + n] = spread_bias(vectors_ref[:, 80 + 32 * n:112 + 32 * n], 64)


def prepare_weights(place, first, kernels, vectors):
    shapes = [(512, 256), (192, 256), (96, 768), (128, 1792), (2, 192, 256), (192, 256), (128, 256), (128, 32)]
    vmem = pl.BlockSpec(memory_space=pltpu.VMEM)
    return pl.pallas_call(
        weights_kernel,
        out_shape=[jax.ShapeDtypeStruct(s, BF16) for s in shapes]
        + [jax.ShapeDtypeStruct((8, 64), F32), jax.ShapeDtypeStruct((7, 64, 128), F32),
           jax.ShapeDtypeStruct((256, 2 * FINE), BF16), jax.ShapeDtypeStruct((2, 8, 128), F32)],
        in_specs=[pl.BlockSpec(memory_space=pltpu.SMEM)] + [vmem] * 3,
        out_specs=[vmem] * 12,
        scratch_shapes=[pltpu.VMEM((48, 256), F32), pltpu.VMEM((48, 512), F32), pltpu.VMEM((32, 1792), F32)],
        compiler_params=pltpu.CompilerParams(vmem_limit_bytes=24 * 2**20),
        cost_estimate=pl.CostEstimate(flops=10**7, bytes_accessed=2 * 10**6, transcendentals=0),
        name="weights",
    )(place, first, kernels, vectors)


def pick(flag, yes, no):
    rows = yes.shape[0] // 8
    return jnp.where((jnp.concatenate([flag] * rows, axis=0) if rows > 1 else flag) > 0.5, yes, no)


def edges_kernel(flags_ref, low_ref, a_ref, mid_ref, b_ref, high_ref, left_ref, right_ref, cells_ref):
    odd_y = flags_ref[0]
    for x in range(8):
        planes = [
            jnp.concatenate([low_ref[8 * g + x], ref[x], high_ref[8 * g + x]], axis=0).astype(F32)
            for g, ref in enumerate((a_ref, mid_ref, b_ref))
        ]
        cells_ref[32 * x:32 * x + 32] = pick(odd_y, planes[2], planes[0])
        cells_ref[32 * (8 + x):32 * (8 + x) + 32] = planes[1]
        cells_ref[32 * (16 + x):32 * (16 + x) + 32] = pick(odd_y, planes[0], planes[2])
    left = [jnp.zeros((24, 128), F32)] * 2
    right = [jnp.zeros((24, 128), F32)] * 2
    lane = iota((24, 128), 1)
    for y in range(32):
        b, at = y % 2, 8 * (y // 2)
        rows = cells_ref[pl.ds(y, 24, stride=32), :]
        inside = (lane >= at) & (lane < at + 8)
        left[b] = jnp.where(inside, pltpu.roll(rows, at, 1) if at else rows, left[b])
        right[b] = jnp.where(inside, pltpu.roll(rows, (at + 8) % 128, 1) if at < 120 else rows, right[b])
    left_ref[...] = jnp.concatenate(left, axis=0).astype(BF16)
    right_ref[...] = jnp.concatenate(right, axis=0).astype(BF16)


def pack_edges(flags, *pieces):
    vmem = pl.BlockSpec(memory_space=pltpu.VMEM)
    return pl.pallas_call(
        edges_kernel,
        out_shape=[jax.ShapeDtypeStruct((48, 128), BF16)] * 2 + [jax.ShapeDtypeStruct((768, 128), F32)],
        in_specs=[vmem] * 6,
        out_specs=[vmem] * 3,
        compiler_params=pltpu.CompilerParams(vmem_limit_bytes=8 * 2**20),
        name="edges",
    )(flags, *pieces)


def sample_kernel(cells_ref, sz_ref, phase_ref, even_ref, odd_ref):
    for at in range(0, 768, 256):
        sampled = jnp.dot(cells_ref[at:at + 256].astype(BF16), sz_ref[...], preferred_element_type=F32)
        even_ref[at:at + 256] = sampled[:, 0:128]
        odd_ref[at:at + 256] = sampled[:, 128:256]
    for y in range(32):
        to = ROW * (y // 2)
        for e, ref in enumerate((even_ref, odd_ref)):
            phase_ref[2 * (y % 2) + e, :, to:to + ROW] = ref[pl.ds(y, 24, stride=32), :][:, 0:ROW]


def sample(cells, sz):
    vmem = pl.BlockSpec(memory_space=pltpu.VMEM)
    return pl.pallas_call(
        sample_kernel,
        out_shape=jax.ShapeDtypeStruct((4, 24, FINE), F32),
        in_specs=[vmem] * 2,
        out_specs=vmem,
        scratch_shapes=[pltpu.VMEM((768, 128), F32), pltpu.VMEM((768, 128), F32)],
        compiler_params=pltpu.CompilerParams(vmem_limit_bytes=8 * 2**20),
        cost_estimate=pl.CostEstimate(flops=10**8, bytes_accessed=10**6, transcendentals=0),
        name="sample",
    )(cells, sz)


def chunks(width):
    return [slice(at, min(at + 256, width)) for at in range(0, width, 256)]


def moved(values, step):
    return pltpu.roll(values, step % values.shape[1], 1) if step else values


def shifted(values, start, width):
    whole = start // 128 * 128
    if start >= 0 and whole + width + 128 <= values.shape[1]:
        values, start = values[:, whole:whole + width + 128], start - whole
    return moved(values, -start)[:, 0:width]


def window(values, start, width):
    rows = []
    for b in range(2):
        even = values[32 * b:32 * b + 16]
        odd = values[32 * b + 16:32 * b + 32]
        rows.append(jnp.concatenate([moved(odd, 1), even, odd, moved(even, -1)], axis=0))
    return jnp.concatenate([shifted(rows[1], start - ROW, width), shifted(rows[0], start, width),
                            shifted(rows[1], start, width), shifted(rows[0], start + ROW, width)], axis=0)


def neighbours(values, start, width):
    rows = jnp.concatenate([moved(values, 1), values, moved(values, -1)], axis=0)
    return jnp.concatenate([shifted(rows, start + ROW * step, width) for step in (-1, 0, 1)], axis=0)


def two_planes(sums_a, sums_b, acc_ref, part):
    done_a = acc_ref[1, :, part] + sums_a[128:192]
    done_b = acc_ref[0, :, part] + sums_a[64:128] + sums_b[128:192]
    acc_ref[1, :, part] = sums_a[0:64] + sums_b[64:128]
    acc_ref[0, :, part] = sums_b[0:64]
    return done_a, done_b


def paired_dots(w_ref, ref_a, ref_b, width):
    whole = width // 256 * 256
    for at in range(0, whole, 256):
        part = slice(at, at + 256)
        yield part, [jnp.dot(w_ref[...], ref[:, part], preferred_element_type=F32) for ref in (ref_a, ref_b)]
    if whole < width:
        part = slice(whole, width)
        both = jnp.dot(w_ref[...], jnp.concatenate([ref_a[:, part], ref_b[:, part]], axis=1), preferred_element_type=F32)
        yield part, [both[:, 0:width - whole], both[:, width - whole:]]


def wide(bias, values):
    rows, columns = values.shape
    bias = jnp.concatenate([bias] * (columns // 128), axis=1) if columns > 128 else bias
    return jnp.concatenate([bias] * (rows // bias.shape[0]), axis=0) if rows > bias.shape[0] else bias


def network_kernel(flags_ref, center_ref, edge_a_ref, edge_b_ref,
                   w1_ref, w2_ref, w4_ref, w5_ref, w7_ref, w8_ref, w6_ref, w9_ref, bias_ref, expand_ref,
                   out_ref,
                   col0_ref, first_ref, slot_a_ref, slot_b_ref, acc_ref,
                   skip_ref, pool_ref, col4_ref, col5_ref, col7_ref, raised_ref, merged_ref, col8_ref, flat_ref, last_ref):
    odd_z = flags_ref[1]
    edge_a = edge_a_ref[...].astype(F32)
    edge_b = edge_b_ref[...].astype(F32)
    edges = jnp.concatenate([pick(odd_z, edge_b, edge_a), pick(odd_z, edge_a, edge_b)], axis=1).astype(BF16)
    placed = [jnp.dot(edges, expand_ref[:, FINE * e:FINE * e + FINE], preferred_element_type=F32) for e in range(2)]
    rows = []
    for b in range(2):
        even, odd = [center_ref[2 * b + e] + placed[e][24 * b:24 * b + 24] for e in range(2)]
        rows.append([moved(odd, 1), even, odd, moved(even, -1)])
    for g in range(3):
        even, odd = [
            jnp.concatenate([part[8 * g:8 * g + 8] for part in rows[b]], axis=0).astype(BF16) for b in range(2)
        ]
        col0_ref[128 * g:128 * g + 128] = jnp.concatenate([moved(odd, ROW), even, odd, moved(even, -ROW)], axis=0)

    bias = bias_ref[0]
    w1_first_ref = w1_ref.at[0:128, 0:128]
    for part, sums in paired_dots(w1_ref, col0_ref.at[0:256], col0_ref.at[128:384], FINE):
        for g in range(2):
            values = leaky(sums[g] + wide(bias, sums[g])).astype(BF16)
            first_ref[8 * g:8 * g + 8, :, part] = values.reshape(8, 64, values.shape[1])
    for part in chunks(FINE):
        sums = jnp.dot(w1_first_ref[...], col0_ref[256:384, part], preferred_element_type=F32)
        values = leaky(sums + wide(bias, sums)).astype(BF16)
        first_ref[16:18, :, part] = values.reshape(2, 64, values.shape[1])

    bias_second = bias_ref[1]

    def gather_first(j, slot_ref):
        for a in range(2):
            slot_ref[a] = window(first_ref[2 * j + a], 0, FINE)

    def skipped_planes(j, slot_ref):
        for part, sums in paired_dots(w2_ref, slot_ref.at[0], slot_ref.at[1], FINE):
            top = None
            for a, done in enumerate(two_planes(*sums, acc_ref, part)):
                values = leaky(done + wide(bias_second, done))
                skip_ref[j, 64 * a:64 * a + 64, part] = values.astype(BF16)
                highest = jnp.max(values.reshape(4, 16, values.shape[1]), axis=0)
                top = highest if top is None else jnp.maximum(top, highest)
            pool_ref[j, :, part] = top.astype(BF16)

    gather_first(0, slot_a_ref)

    def two_steps(t, carry):
        gather_first(2 * t + 1, slot_b_ref)
        skipped_planes(2 * t, slot_a_ref)
        gather_first(2 * t + 2, slot_a_ref)
        skipped_planes(2 * t + 1, slot_b_ref)
        return carry

    lax.fori_loop(0, 4, two_steps, 0)
    skipped_planes(8, slot_a_ref)

    for s in range(8):
        col4_ref[144 * s:144 * s + 144] = neighbours(pool_ref[s + 1], COARSE, COARSE_WIDTH)
    col4_ref[1152:1200] = jnp.zeros((48, COARSE_WIDTH), BF16)
    for d in range(4):
        for a in range(2):
            col7_ref[2 * d + a] = window(skip_ref[d + 3, 64 * a:64 * a + 64], RAISED, RAISED_WIDTH)
    for j in range(4):
        for part, sums in paired_dots(w7_ref.at[1], col7_ref.at[2 * j], col7_ref.at[2 * j + 1], RAISED_WIDTH):
            for a, done in enumerate(two_planes(*sums, acc_ref, part)):
                if j > 0:
                    merged_ref[2 * j + a - 2, :, part] = done

    bias_coarse = bias_ref[5, 0:32]
    parts = [[], []]
    for _, sums in paired_dots(w4_ref, col4_ref.at[0:768], col4_ref.at[432:1200], COARSE_WIDTH):
        for m in range(2):
            parts[m].append(leaky(sums[m] + wide(bias_coarse, sums[m])).astype(BF16))
    for m in range(2):
        values = jnp.concatenate(parts[m], axis=1)
        for p in range(3):
            at = 288 * (3 * m + p)
            col5_ref[at:at + 288] = neighbours(values[32 * p:32 * p + 32], RAISED - COARSE, RAISED_WIDTH)
    col5_ref[1728:1792] = jnp.zeros((64, RAISED_WIDTH), BF16)

    bias_deeper = bias_ref[6, 0:32]
    bias_raised = bias_ref[2]
    parts = []
    for part in chunks(RAISED_WIDTH):
        sums = jnp.dot(w5_ref[...], col5_ref[:, part], preferred_element_type=F32)
        parts.append(leaky(sums + wide(bias_deeper, sums)).astype(BF16))
    deeper = jnp.concatenate(parts, axis=1)
    for d in range(4):
        parts = []
        for part in chunks(RAISED_WIDTH):
            sums = jnp.dot(w6_ref[...], deeper[32 * d:32 * d + 32, part], preferred_element_type=F32)
            parts.append(leaky(sums + wide(bias_raised, sums)).astype(BF16))
        values = jnp.concatenate(parts, axis=1)
        for a in range(2):
            raised_ref[2 * d + a] = window(values[64 * a:64 * a + 64], 0, RAISED_WIDTH)

    bias_joined = bias_ref[3]
    for j in range(4):
        parts = [[], []]
        for part, sums in paired_dots(w7_ref.at[0], raised_ref.at[2 * j], raised_ref.at[2 * j + 1], RAISED_WIDTH):
            for a, done in enumerate(two_planes(*sums, acc_ref, part)):
                if j > 0:
                    done = done + merged_ref[2 * j + a - 2, :, part]
                    parts[a].append(leaky(done + wide(bias_joined, done)).astype(BF16))
        if j > 0:
            for a in range(2):
                values = jnp.concatenate(parts[a], axis=1)
                col8_ref[2 * j + a - 2] = window(values, FINAL - RAISED, FINAL_WIDTH)

    bias_final = bias_ref[4]
    output_matrix = w9_ref[...].astype(BF16)
    for j in range(3):
        for part, sums in paired_dots(w8_ref, col8_ref.at[2 * j], col8_ref.at[2 * j + 1], FINAL_WIDTH):
            done = two_planes(*sums, acc_ref, part)
            if j > 0:
                for a in range(2):
                    values = leaky(done[a] + wide(bias_final, done[a])).astype(BF16)
                    predicted = jnp.dot(output_matrix, values, preferred_element_type=F32)
                    to = 4 * (j - 1) + 2 * a
                    flat_ref[0, to:to + 2, part] = predicted[0:2]
                    flat_ref[1, to:to + 2, part] = predicted[2:4]

    for y in range(8):
        at = ROW * (y + 4) - FINAL + 4
        last_ref[8 * y:8 * y + 8, 0:64] = flat_ref[0, :, at:at + 64]
        last_ref[8 * y:8 * y + 8, 64:128] = flat_ref[1, :, at:at + 64]
    old = iota((128, 128), 0)
    turns = (2 * (old % 64) + old // 64 == iota((128, 128), 1)).astype(F32)
    result = jnp.dot(last_ref[...], turns, preferred_element_type=F32, precision=lax.Precision.HIGHEST)
    for y in range(8):
        for x in range(4):
            at = 8 * y + 2 * x
            out_ref[x, 2 * y:2 * y + 2, :] = result[at:at + 2]


def network(flags, center, edge_a, edge_b, weights):
    vmem = pl.BlockSpec(memory_space=pltpu.VMEM)
    scratch = [
        ((384, FINE), BF16), ((18, 64, FINE), BF16), ((2, 256, FINE), BF16), ((2, 256, FINE), BF16),
        ((2, 64, FINE), F32), ((9, 128, FINE), BF16), ((9, 16, FINE), BF16),
        ((1200, COARSE_WIDTH), BF16), ((1792, RAISED_WIDTH), BF16), ((8, 256, RAISED_WIDTH), BF16),
        ((8, 256, RAISED_WIDTH), BF16), ((6, 64, RAISED_WIDTH), F32), ((6, 256, FINAL_WIDTH), BF16),
        ((2, 8, FINAL_WIDTH), F32), ((64, 128), F32),
    ]
    operands = (flags, center, edge_a, edge_b, *weights)
    return pl.pallas_call(
        network_kernel,
        out_shape=jax.ShapeDtypeStruct((4, 16, 128), F32),
        in_specs=[vmem] * len(operands),
        out_specs=vmem,
        scratch_shapes=[pltpu.VMEM(shape, kind) for shape, kind in scratch],
        compiler_params=pltpu.CompilerParams(vmem_limit_bytes=50 * 2**20),
        cost_estimate=pl.CostEstimate(flops=4 * 10**9, bytes_accessed=4 * 10**6, transcendentals=0),
        name="network",
    )(*operands)


def ring(size, step):
    return [(i, (i + step) % size) for i in range(size)]


def partner(i, size, first):
    return (i + 1 if (i % 2 == 1) == first else i - 1) % size


def swaps_y(first):
    return [(gx, 2 * partner(gx // 2, 4, first) + gx % 2) for gx in range(8)]


def swaps_z(first):
    pairs = []
    for gx in range(8):
        for gz in range(8):
            to = partner(gx % 2 * 8 + gz, 16, first)
            pairs.append((gx * 8 + gz, (gx // 2 * 2 + to // 8) * 8 + to % 8))
    return pairs


def exchange(density, half, pack):
    other = lax.ppermute(density, "gx", [(i, i ^ 1) for i in range(8)])
    other, flags = yield other
    mid = jnp.concatenate([jnp.where(half == 0, density, other), jnp.where(half == 0, other, density)], axis=0)
    a = lax.ppermute(mid, "gx", swaps_y(True))
    b = lax.ppermute(mid, "gx", swaps_y(False))
    high = jnp.concatenate([a[:, 8:], mid[:, 8:], b[:, 8:]], axis=0)
    low = jnp.concatenate([a[:, :8], mid[:, :8], b[:, :8]], axis=0)
    low, high = lax.ppermute(high, "gy", ring(8, 1)), lax.ppermute(low, "gy", ring(8, -1))
    left, right, cells = pack(flags, low, a, mid, b, high)
    odd = lax.axis_index("gz") % 2 == 1
    edge_a = lax.ppermute(jnp.where(odd, right, left), ("gx", "gz"), swaps_z(True))
    edge_b = lax.ppermute(jnp.where(odd, left, right), ("gx", "gz"), swaps_z(False))
    yield edge_a, edge_b, cells


def body(density, first_kernel, first_bias, second_kernel, second_bias, coarse_kernel, coarse_bias, deeper_kernel,
         deeper_bias, upward_kernel, upward_bias, joined_kernel, joined_bias, final_kernel, final_bias, output_weight):
    half = (lax.axis_index("gx") % 2).astype(jnp.int32)
    place = jnp.stack([half, lax.axis_index("gx") // 2 % 2, lax.axis_index("gz") % 2]).astype(jnp.int32)
    steps = exchange(density, half, pack_edges)
    other = next(steps)
    kernels = jnp.concatenate([
        jnp.concatenate([second_kernel, final_kernel], axis=4).reshape(432, 32), joined_kernel.reshape(432, 32),
        jnp.swapaxes(coarse_kernel, 3, 4).reshape(432, 32), deeper_kernel.reshape(864, 32), upward_kernel.reshape(128, 32),
    ], axis=0)
    vectors = jnp.concatenate([first_bias, second_bias, upward_bias, joined_bias, final_bias, coarse_bias, deeper_bias,
                               output_weight.astype(F32)]).reshape(1, 160)
    weights = prepare_weights(place, first_kernel.reshape(27, 16), kernels, vectors)
    other, weights = lax.optimization_barrier((other, weights))
    *weights, flags = weights
    sz = weights.pop(6)
    edge_a, edge_b, cells = steps.send((other, flags))
    return network(flags, sample(cells, sz), edge_a, edge_b, weights)


def solution(mesh):
    placed = (P("gx", "gy", "gz"),) + (P(),) * 15
    return jax.shard_map(body, mesh=mesh, in_specs=placed, out_specs=P("gx", "gy", "gz"), check_vma=False)
```

```python
import functools

import jax
import jax.numpy as jnp
from jax import lax
from jax.experimental import pallas as pl
from jax.experimental.pallas import tpu as pltpu
from jax.sharding import PartitionSpec as P

F32 = jnp.float32
BF16 = jnp.bfloat16
ROW = 72
FINE = 1152
COARSE, COARSE_WIDTH = 128, 896
RAISED, RAISED_WIDTH = 200, 768
FINAL, FINAL_WIDTH = 272, 640


def leaky(values):
    return jnp.maximum(values, 0.2 * values)


def iota(shape, dim):
    return lax.broadcasted_iota(jnp.int32, shape, dim)


def spread_bias(bias, rows):
    count = bias.shape[1]
    match = iota((rows, count), 0) % count == iota((rows, count), 1)
    return jnp.broadcast_to(jnp.sum(jnp.where(match, bias, 0.0), axis=1, keepdims=True), (rows, 128))


def weights_kernel(place_ref, first_ref, *refs):
    kernels_ref, vectors_ref = refs[:2]
    (w1_ref, w2_ref, w4_ref, w5_ref, w7_ref, w8_ref, sz_ref, w6_ref, w9_ref, bias_ref, expand_ref, flags_ref) = refs[2:14]
    fine_ref, joint_ref, deeper_base_ref = refs[14:]

    tap = iota((27, 256), 0)
    lane = iota((27, 256), 1)
    place = (tap % 3) * 64 + (tap // 3 % 3) * 16 + tap // 9
    base = lax.dot_general(first_ref[...], (place == lane).astype(BF16), (((0,), (0,)), ((), ())),
                           preferred_element_type=F32)
    base = jnp.where(place_ref[0] == 0, base, pltpu.roll(base, 4, 1))
    old = iota((256, 256), 0)
    new = iota((256, 256), 1)
    order = (old % 16 // 8) * 128 + (old // 16 % 4) * 32 + (old // 64) * 8 + old % 8
    permute = (order == new).astype(BF16)
    for x in range(8):
        rows = jnp.concatenate(
            [pltpu.roll(base, x + 16 * b + 64 * e, 1) if x + b + e else base for b in range(2) for e in range(2)], axis=0)
        w1_ref[64 * x:64 * x + 64] = jnp.dot(rows.astype(BF16), permute, preferred_element_type=F32).astype(BF16)

    row = iota((128, 256), 0)
    sz_ref[...] = (iota((128, 256), 1) == (row % 2) * 128 + row // 2 + 4).astype(BF16)
    row = iota((256, 2 * FINE), 0)
    cell = row % 8 + 136 * (row // 128)
    target = (cell % 2) * FINE + (row % 128 // 8) * ROW + cell // 2
    expand_ref[...] = (iota((256, 2 * FINE), 1) == target).astype(BF16)
    for n in range(2):
        flags_ref[n] = jnp.full((8, 128), place_ref[n + 1].astype(F32))

    for side, target in ((0, w2_ref), (1, w8_ref)):
        fine_ref[...] = jnp.zeros_like(fine_ref)
        for t in range(27):
            at = (t // 3 % 3) * 64 + (t % 3) * 16
            fine_ref[16 * (t // 9):16 * (t // 9) + 16, at:at + 16] = kernels_ref[
                16 * t:16 * t + 16, 16 * side:16 * side + 16].astype(F32)
        for u in range(3):
            block = fine_ref[16 * u:16 * u + 16]
            for n in range(4):
                move = (n // 2) * 64 + (n % 2) * 16
                at = 64 * u + 16 * n
                target[at:at + 16] = (pltpu.roll(block, move, 1) if n else block).astype(BF16)

    joint_ref[...] = jnp.zeros_like(joint_ref)
    for t in range(27):
        piece = kernels_ref[432 + 16 * t:448 + 16 * t].astype(F32)
        for side in range(2):
            at = side * 256 + (t // 3 % 3) * 64 + (t % 3) * 16
            joint_ref[16 * (t // 9):16 * (t // 9) + 16, at:at + 16] = piece[:, 16 * side:16 * side + 16]
    for u in range(3):
        block = joint_ref[16 * u:16 * u + 16]
        for n in range(4):
            move = (n // 2) * 64 + (n % 2) * 16
            at = 64 * u + 16 * n
            rows = (pltpu.roll(block, move, 1) if n else block).astype(BF16)
            for side in range(2):
                w7_ref[side, at:at + 16] = rows[:, 256 * side:256 * side + 256]

    same = (iota((432, 768), 0) == iota((432, 768), 1)).astype(BF16)
    block = lax.dot_general(kernels_ref[864:1296], same, (((0,), (0,)), ((), ())), preferred_element_type=F32)
    for p in range(3):
        w4_ref[32 * p:32 * p + 32] = (pltpu.roll(block, 144 * p, 1) if p else block).astype(BF16)
    deeper_base_ref[...] = jnp.zeros_like(deeper_base_ref)
    for t in range(27):
        deeper_base_ref[:, 32 * t:32 * t + 32] = kernels_ref[1296 + 32 * t:1328 + 32 * t].astype(F32)
    block = deeper_base_ref[...]
    for p in range(4):
        w5_ref[32 * p:32 * p + 32] = (pltpu.roll(block, 288 * p, 1) if p else block).astype(BF16)

    w6_ref[...] = kernels_ref[2160:2288]
    spread = (iota((16, 64), 0) == iota((16, 64), 1) % 16).astype(BF16)
    row_weights = jnp.dot(vectors_ref[:, 144:160].astype(BF16), spread, preferred_element_type=F32)
    row = iota((8, 64), 0)
    group = iota((8, 64), 1) // 16
    chosen = (row % 2 == group // 2) & (row // 2 == group % 2)
    w9_ref[...] = jnp.where(chosen, row_weights, 0.0)
    for n in range(5):
        bias_ref[n] = spread_bias(vectors_ref[:, 16 * n:16 * n + 16], 64)
    for n in range(2):
        bias_ref[5 + n] = spread_bias(vectors_ref[:, 80 + 32 * n:112 + 32 * n], 64)


def prepare_weights(place, first, kernels, vectors):
    shapes = [(512, 256), (192, 256), (96, 768), (128, 1792), (2, 192, 256), (192, 256), (128, 256), (128, 32)]
    vmem = pl.BlockSpec(memory_space=pltpu.VMEM)
    return pl.pallas_call(
        weights_kernel,
        out_shape=[jax.ShapeDtypeStruct(s, BF16) for s in shapes]
        + [jax.ShapeDtypeStruct((8, 64), F32), jax.ShapeDtypeStruct((7, 64, 128), F32),
           jax.ShapeDtypeStruct((256, 2 * FINE), BF16), jax.ShapeDtypeStruct((2, 8, 128), F32)],
        in_specs=[pl.BlockSpec(memory_space=pltpu.SMEM)] + [vmem] * 3,
        out_specs=[vmem] * 12,
        scratch_shapes=[pltpu.VMEM((48, 256), F32), pltpu.VMEM((48, 512), F32), pltpu.VMEM((32, 1792), F32)],
        compiler_params=pltpu.CompilerParams(vmem_limit_bytes=24 * 2**20),
        cost_estimate=pl.CostEstimate(flops=10**7, bytes_accessed=2 * 10**6, transcendentals=0),
        name="weights",
    )(place, first, kernels, vectors)


def pick(flag, yes, no):
    rows = yes.shape[0] // 8
    return jnp.where((jnp.concatenate([flag] * rows, axis=0) if rows > 1 else flag) > 0.5, yes, no)


def edges_kernel(flags_ref, low_ref, a_ref, mid_ref, b_ref, high_ref, left_ref, right_ref, cells_ref):
    odd_y = flags_ref[0]
    for x in range(8):
        planes = [
            jnp.concatenate([low_ref[8 * g + x], ref[x], high_ref[8 * g + x]], axis=0).astype(F32)
            for g, ref in enumerate((a_ref, mid_ref, b_ref))
        ]
        cells_ref[32 * x:32 * x + 32] = pick(odd_y, planes[2], planes[0])
        cells_ref[32 * (8 + x):32 * (8 + x) + 32] = planes[1]
        cells_ref[32 * (16 + x):32 * (16 + x) + 32] = pick(odd_y, planes[0], planes[2])
    left = [jnp.zeros((24, 128), F32)] * 2
    right = [jnp.zeros((24, 128), F32)] * 2
    lane = iota((24, 128), 1)
    for y in range(32):
        b, at = y % 2, 8 * (y // 2)
        rows = cells_ref[pl.ds(y, 24, stride=32), :]
        inside = (lane >= at) & (lane < at + 8)
        left[b] = jnp.where(inside, pltpu.roll(rows, at, 1) if at else rows, left[b])
        right[b] = jnp.where(inside, pltpu.roll(rows, (at + 8) % 128, 1) if at < 120 else rows, right[b])
    left_ref[...] = jnp.concatenate(left, axis=0).astype(BF16)
    right_ref[...] = jnp.concatenate(right, axis=0).astype(BF16)


def pack_edges(flags, *pieces):
    vmem = pl.BlockSpec(memory_space=pltpu.VMEM)
    return pl.pallas_call(
        edges_kernel,
        out_shape=[jax.ShapeDtypeStruct((48, 128), BF16)] * 2 + [jax.ShapeDtypeStruct((768, 128), F32)],
        in_specs=[vmem] * 6,
        out_specs=[vmem] * 3,
        compiler_params=pltpu.CompilerParams(vmem_limit_bytes=8 * 2**20),
        name="edges",
    )(flags, *pieces)


def sample_kernel(cells_ref, sz_ref, phase_ref, even_ref, odd_ref):
    for at in range(0, 768, 256):
        sampled = jnp.dot(cells_ref[at:at + 256].astype(BF16), sz_ref[...], preferred_element_type=F32)
        even_ref[at:at + 256] = sampled[:, 0:128]
        odd_ref[at:at + 256] = sampled[:, 128:256]
    for y in range(32):
        to = ROW * (y // 2)
        for e, ref in enumerate((even_ref, odd_ref)):
            phase_ref[2 * (y % 2) + e, :, to:to + ROW] = ref[pl.ds(y, 24, stride=32), :][:, 0:ROW]


def sample(cells, sz):
    vmem = pl.BlockSpec(memory_space=pltpu.VMEM)
    return pl.pallas_call(
        sample_kernel,
        out_shape=jax.ShapeDtypeStruct((4, 24, FINE), F32),
        in_specs=[vmem] * 2,
        out_specs=vmem,
        scratch_shapes=[pltpu.VMEM((768, 128), F32), pltpu.VMEM((768, 128), F32)],
        compiler_params=pltpu.CompilerParams(vmem_limit_bytes=8 * 2**20),
        cost_estimate=pl.CostEstimate(flops=10**8, bytes_accessed=10**6, transcendentals=0),
        name="sample",
    )(cells, sz)


def chunks(width):
    return [slice(at, min(at + 256, width)) for at in range(0, width, 256)]


def moved(values, step):
    return pltpu.roll(values, step % values.shape[1], 1) if step else values


def shifted(values, start, width):
    whole = start // 128 * 128
    if start >= 0 and whole + width + 128 <= values.shape[1]:
        values, start = values[:, whole:whole + width + 128], start - whole
    return moved(values, -start)[:, 0:width]


def window_steps(values, start, width, target_ref):
    for b in range(2):
        even = values[32 * b:32 * b + 16]
        odd = values[32 * b + 16:32 * b + 32]
        rows = jnp.concatenate([moved(odd, 1), even, odd, moved(even, -1)], axis=0)
        at = 64 + 64 * b
        target_ref[at:at + 64] = shifted(rows, start, width)
        yield
        at = 192 - 192 * b
        target_ref[at:at + 64] = shifted(rows, start + ROW - 2 * ROW * b, width)
        yield


def together(*steps):
    steps = list(steps)
    while steps:
        for work in list(steps):
            if next(work, work) is work:
                steps.remove(work)


def neighbours(values, start, width):
    rows = jnp.concatenate([moved(values, 1), values, moved(values, -1)], axis=0)
    return jnp.concatenate([shifted(rows, start + ROW * step, width) for step in (-1, 0, 1)], axis=0)


def two_planes(sums_a, sums_b, acc_ref, part):
    done_a = acc_ref[1, :, part] + sums_a[128:192]
    done_b = acc_ref[0, :, part] + sums_a[64:128] + sums_b[128:192]
    acc_ref[1, :, part] = sums_a[0:64] + sums_b[64:128]
    acc_ref[0, :, part] = sums_b[0:64]
    return done_a, done_b


def paired_dots(w_ref, ref_a, ref_b, width):
    whole = width // 256 * 256
    for at in range(0, whole, 256):
        part = slice(at, at + 256)
        yield part, [jnp.dot(w_ref[...], ref[:, part], preferred_element_type=F32) for ref in (ref_a, ref_b)]
    if whole < width:
        part = slice(whole, width)
        both = jnp.dot(w_ref[...], jnp.concatenate([ref_a[:, part], ref_b[:, part]], axis=1), preferred_element_type=F32)
        yield part, [both[:, 0:width - whole], both[:, width - whole:]]


def wide(bias, values):
    rows, columns = values.shape
    bias = jnp.concatenate([bias] * (columns // 128), axis=1) if columns > 128 else bias
    return jnp.concatenate([bias] * (rows // bias.shape[0]), axis=0) if rows > bias.shape[0] else bias


def network_kernel(flags_ref, center_ref, edge_a_ref, edge_b_ref,
                   w1_ref, w2_ref, w4_ref, w5_ref, w7_ref, w8_ref, w6_ref, w9_ref, bias_ref, expand_ref,
                   out_ref,
                   col0_ref, first_ref, slot_a_ref, slot_b_ref, acc_ref, last_acc_ref,
                   skip_ref, pool_ref, col4_ref, col5_ref, col7_ref, raised_ref, merged_ref, col8_ref, flat_ref, last_ref):
    odd_z = flags_ref[1]
    edge_a = edge_a_ref[...].astype(F32)
    edge_b = edge_b_ref[...].astype(F32)
    edges = jnp.concatenate([pick(odd_z, edge_b, edge_a), pick(odd_z, edge_a, edge_b)], axis=1).astype(BF16)
    placed = [jnp.dot(edges, expand_ref[:, FINE * e:FINE * e + FINE], preferred_element_type=F32) for e in range(2)]
    rows = []
    for b in range(2):
        even, odd = [center_ref[2 * b + e] + placed[e][24 * b:24 * b + 24] for e in range(2)]
        rows.append([moved(odd, 1), even, odd, moved(even, -1)])
    for g in range(3):
        even, odd = [
            jnp.concatenate([part[8 * g:8 * g + 8] for part in rows[b]], axis=0).astype(BF16) for b in range(2)
        ]
        col0_ref[128 * g:128 * g + 128] = jnp.concatenate([moved(odd, ROW), even, odd, moved(even, -ROW)], axis=0)

    bias = bias_ref[0]
    w1_first_ref = w1_ref.at[0:128, 0:128]
    for part, sums in paired_dots(w1_ref, col0_ref.at[0:256], col0_ref.at[128:384], FINE):
        for g in range(2):
            values = leaky(sums[g] + wide(bias, sums[g])).astype(BF16)
            first_ref[8 * g:8 * g + 8, :, part] = values.reshape(8, 64, values.shape[1])
    for part in chunks(FINE):
        sums = jnp.dot(w1_first_ref[...], col0_ref[256:384, part], preferred_element_type=F32)
        values = leaky(sums + wide(bias, sums)).astype(BF16)
        first_ref[16:18, :, part] = values.reshape(2, 64, values.shape[1])

    bias_second = bias_ref[1]

    def gather_first(j, slot_ref):
        for a in range(2):
            yield from window_steps(first_ref[2 * j + a], 0, FINE, slot_ref.at[a])

    def skipped_planes(j, slot_ref):
        for part, sums in paired_dots(w2_ref, slot_ref.at[0], slot_ref.at[1], FINE):
            yield
            top = None
            for a, done in enumerate(two_planes(*sums, acc_ref, part)):
                values = leaky(done + wide(bias_second, done))
                skip_ref[j, 64 * a:64 * a + 64, part] = values.astype(BF16)
                highest = jnp.max(values.reshape(4, 16, values.shape[1]), axis=0)
                top = highest if top is None else jnp.maximum(top, highest)
            pool_ref[j, :, part] = top.astype(BF16)
            yield

    def gather_pool(planes):
        for s in planes:
            col4_ref[144 * s:144 * s + 144] = neighbours(pool_ref[s + 1], COARSE, COARSE_WIDTH)
            yield

    together(gather_first(0, slot_a_ref))

    def two_steps(t, carry):
        together(skipped_planes(2 * t, slot_a_ref), gather_first(2 * t + 1, slot_b_ref))
        together(skipped_planes(2 * t + 1, slot_b_ref), gather_first(2 * t + 2, slot_a_ref))
        return carry

    lax.fori_loop(0, 4, two_steps, 0)
    col4_ref[1152:1200] = jnp.zeros((48, COARSE_WIDTH), BF16)
    col5_ref[1728:1792] = jnp.zeros((64, RAISED_WIDTH), BF16)
    together(skipped_planes(8, slot_a_ref), gather_pool(range(7)))
    together(gather_pool([7]))

    bias_coarse = bias_ref[5, 0:32]
    coarse_parts = [[], []]

    def coarse_planes():
        for _, sums in paired_dots(w4_ref, col4_ref.at[0:768], col4_ref.at[432:1200], COARSE_WIDTH):
            yield
            for m in range(2):
                coarse_parts[m].append(leaky(sums[m] + wide(bias_coarse, sums[m])).astype(BF16))
            yield

    def gather_skipped(planes):
        for d in planes:
            for a in range(2):
                yield from window_steps(skip_ref[d + 3, 64 * a:64 * a + 64], RAISED, RAISED_WIDTH, col7_ref.at[2 * d + a])

    together(coarse_planes(), gather_skipped(range(2)))

    def gather_coarse():
        for m in range(2):
            values = jnp.concatenate(coarse_parts[m], axis=1)
            for p in range(3):
                at = 288 * (3 * m + p)
                col5_ref[at:at + 288] = neighbours(values[32 * p:32 * p + 32], RAISED - COARSE, RAISED_WIDTH)
                yield

    def merged_skipped(pairs):
        for j in pairs:
            for part, sums in paired_dots(w7_ref.at[1], col7_ref.at[2 * j], col7_ref.at[2 * j + 1], RAISED_WIDTH):
                yield
                for a, done in enumerate(two_planes(*sums, acc_ref, part)):
                    if j > 0:
                        merged_ref[2 * j + a - 2, :, part] = done
                yield

    together(gather_coarse(), merged_skipped(range(2)))

    bias_deeper = bias_ref[6, 0:32]
    deeper_parts = []

    def deeper_planes():
        for part in chunks(RAISED_WIDTH):
            sums = jnp.dot(w5_ref[...], col5_ref[:, part], preferred_element_type=F32)
            yield
            deeper_parts.append(leaky(sums + wide(bias_deeper, sums)).astype(BF16))
            yield

    together(deeper_planes(), gather_skipped(range(2, 4)))
    deeper = jnp.concatenate(deeper_parts, axis=1)

    bias_raised = bias_ref[2]
    raised_parts = [[], [], [], []]

    def raised_planes(d):
        for part in chunks(RAISED_WIDTH):
            sums = jnp.dot(w6_ref[...], deeper[32 * d:32 * d + 32, part], preferred_element_type=F32)
            yield
            raised_parts[d].append(leaky(sums + wide(bias_raised, sums)).astype(BF16))
            yield

    def gather_raised(d):
        values = jnp.concatenate(raised_parts[d], axis=1)
        for a in range(2):
            yield from window_steps(values[64 * a:64 * a + 64], 0, RAISED_WIDTH, raised_ref.at[2 * d + a])

    bias_joined = bias_ref[3]
    merged_parts = {}

    def merged_planes(j):
        merged_parts[j] = [[], []]
        for part, sums in paired_dots(w7_ref.at[0], raised_ref.at[2 * j], raised_ref.at[2 * j + 1], RAISED_WIDTH):
            yield
            for a, done in enumerate(two_planes(*sums, acc_ref, part)):
                if j > 0:
                    done = done + merged_ref[2 * j + a - 2, :, part]
                    merged_parts[j][a].append(leaky(done + wide(bias_joined, done)).astype(BF16))
            yield

    def gather_merged(j):
        for a in range(2):
            values = jnp.concatenate(merged_parts[j][a], axis=1)
            yield from window_steps(values, FINAL - RAISED, FINAL_WIDTH, col8_ref.at[2 * j + a - 2])

    bias_final = bias_ref[4]
    output_matrix = w9_ref[...].astype(BF16)

    def final_planes(j):
        for part, sums in paired_dots(w8_ref, col8_ref.at[2 * j], col8_ref.at[2 * j + 1], FINAL_WIDTH):
            yield
            done = two_planes(*sums, last_acc_ref, part)
            if j > 0:
                for a in range(2):
                    values = leaky(done[a] + wide(bias_final, done[a])).astype(BF16)
                    predicted = jnp.dot(output_matrix, values, preferred_element_type=F32)
                    to = 4 * (j - 1) + 2 * a
                    flat_ref[0, to:to + 2, part] = predicted[0:2]
                    flat_ref[1, to:to + 2, part] = predicted[2:4]
            yield

    together(raised_planes(0), merged_skipped([2]))
    together(gather_raised(0), raised_planes(1), merged_skipped([3]))
    together(gather_raised(1), raised_planes(2), merged_planes(0))
    together(gather_raised(2), raised_planes(3), merged_planes(1))
    together(gather_raised(3), merged_planes(2), gather_merged(1))
    together(merged_planes(3), gather_merged(2), final_planes(0))
    together(gather_merged(3), final_planes(1))
    together(final_planes(2))

    for y in range(8):
        at = ROW * (y + 4) - FINAL + 4
        last_ref[8 * y:8 * y + 8, 0:64] = flat_ref[0, :, at:at + 64]
        last_ref[8 * y:8 * y + 8, 64:128] = flat_ref[1, :, at:at + 64]
    old = iota((128, 128), 0)
    turns = (2 * (old % 64) + old // 64 == iota((128, 128), 1)).astype(F32)
    result = jnp.dot(last_ref[...], turns, preferred_element_type=F32, precision=lax.Precision.HIGHEST)
    for y in range(8):
        for x in range(4):
            at = 8 * y + 2 * x
            out_ref[x, 2 * y:2 * y + 2, :] = result[at:at + 2]


def network(flags, center, edge_a, edge_b, weights):
    vmem = pl.BlockSpec(memory_space=pltpu.VMEM)
    scratch = [
        ((384, FINE), BF16), ((18, 64, FINE), BF16), ((2, 256, FINE), BF16), ((2, 256, FINE), BF16),
        ((2, 64, FINE), F32), ((2, 64, FINAL_WIDTH), F32), ((9, 128, FINE), BF16), ((9, 16, FINE), BF16),
        ((1200, COARSE_WIDTH), BF16), ((1792, RAISED_WIDTH), BF16), ((8, 256, RAISED_WIDTH), BF16),
        ((8, 256, RAISED_WIDTH), BF16), ((6, 64, RAISED_WIDTH), F32), ((6, 256, FINAL_WIDTH), BF16),
        ((2, 8, FINAL_WIDTH), F32), ((64, 128), F32),
    ]
    operands = (flags, center, edge_a, edge_b, *weights)
    return pl.pallas_call(
        network_kernel,
        out_shape=jax.ShapeDtypeStruct((4, 16, 128), F32),
        in_specs=[vmem] * len(operands),
        out_specs=vmem,
        scratch_shapes=[pltpu.VMEM(shape, kind) for shape, kind in scratch],
        compiler_params=pltpu.CompilerParams(vmem_limit_bytes=50 * 2**20),
        cost_estimate=pl.CostEstimate(flops=4 * 10**9, bytes_accessed=4 * 10**6, transcendentals=0),
        name="network",
    )(*operands)


def ring(size, step):
    return [(i, (i + step) % size) for i in range(size)]


def partner(i, size, first):
    return (i + 1 if (i % 2 == 1) == first else i - 1) % size


def swaps_y(first):
    return [(gx, 2 * partner(gx // 2, 4, first) + gx % 2) for gx in range(8)]


def swaps_z(first):
    pairs = []
    for gx in range(8):
        for gz in range(8):
            to = partner(gx % 2 * 8 + gz, 16, first)
            pairs.append((gx * 8 + gz, (gx // 2 * 2 + to // 8) * 8 + to % 8))
    return pairs


def exchange(density, half, pack):
    other = lax.ppermute(density, "gx", [(i, i ^ 1) for i in range(8)])
    other, flags = yield other
    mid = jnp.concatenate([jnp.where(half == 0, density, other), jnp.where(half == 0, other, density)], axis=0)
    a = lax.ppermute(mid, "gx", swaps_y(True))
    b = lax.ppermute(mid, "gx", swaps_y(False))
    high = jnp.concatenate([a[:, 8:], mid[:, 8:], b[:, 8:]], axis=0)
    low = jnp.concatenate([a[:, :8], mid[:, :8], b[:, :8]], axis=0)
    low, high = lax.ppermute(high, "gy", ring(8, 1)), lax.ppermute(low, "gy", ring(8, -1))
    left, right, cells = pack(flags, low, a, mid, b, high)
    odd = lax.axis_index("gz") % 2 == 1
    edge_a = lax.ppermute(jnp.where(odd, right, left), ("gx", "gz"), swaps_z(True))
    edge_b = lax.ppermute(jnp.where(odd, left, right), ("gx", "gz"), swaps_z(False))
    yield edge_a, edge_b, cells


def body(density, first_kernel, first_bias, second_kernel, second_bias, coarse_kernel, coarse_bias, deeper_kernel,
         deeper_bias, upward_kernel, upward_bias, joined_kernel, joined_bias, final_kernel, final_bias, output_weight):
    half = (lax.axis_index("gx") % 2).astype(jnp.int32)
    place = jnp.stack([half, lax.axis_index("gx") // 2 % 2, lax.axis_index("gz") % 2]).astype(jnp.int32)
    steps = exchange(density, half, pack_edges)
    other = next(steps)
    kernels = jnp.concatenate([
        jnp.concatenate([second_kernel, final_kernel], axis=4).reshape(432, 32), joined_kernel.reshape(432, 32),
        jnp.swapaxes(coarse_kernel, 3, 4).reshape(432, 32), deeper_kernel.reshape(864, 32), upward_kernel.reshape(128, 32),
    ], axis=0)
    vectors = jnp.concatenate([first_bias, second_bias, upward_bias, joined_bias, final_bias, coarse_bias, deeper_bias,
                               output_weight.astype(F32)]).reshape(1, 160)
    weights = prepare_weights(place, first_kernel.reshape(27, 16), kernels, vectors)
    other, weights = lax.optimization_barrier((other, weights))
    *weights, flags = weights
    sz = weights.pop(6)
    edge_a, edge_b, cells = steps.send((other, flags))
    return network(flags, sample(cells, sz), edge_a, edge_b, weights)


def solution(mesh):
    placed = (P("gx", "gy", "gz"),) + (P(),) * 15
    return jax.shard_map(body, mesh=mesh, in_specs=placed, out_specs=P("gx", "gy", "gz"), check_vma=False)
```

```python
import functools

import jax
import jax.numpy as jnp
from jax import lax
from jax.experimental import pallas as pl
from jax.experimental.pallas import tpu as pltpu
from jax.sharding import PartitionSpec as P

F32 = jnp.float32
BF16 = jnp.bfloat16
ROW = 72
FINE = 1152
COARSE, COARSE_WIDTH = 128, 896
RAISED, RAISED_WIDTH = 200, 768
FINAL, FINAL_WIDTH = 272, 640


def leaky(values):
    return jnp.maximum(values, 0.2 * values)


def iota(shape, dim):
    return lax.broadcasted_iota(jnp.int32, shape, dim)


def spread_bias(bias, rows):
    count = bias.shape[1]
    match = iota((rows, count), 0) % count == iota((rows, count), 1)
    return jnp.broadcast_to(jnp.sum(jnp.where(match, bias, 0.0), axis=1, keepdims=True), (rows, 128))


def weights_kernel(place_ref, first_ref, *refs):
    kernels_ref, vectors_ref = refs[:2]
    (w1_ref, w2_ref, w4_ref, w5_ref, w7_ref, w8_ref, sz_ref, w6_ref, w9_ref, bias_ref, expand_ref, flags_ref) = refs[2:14]
    fine_ref, joint_ref, deeper_base_ref = refs[14:]

    tap = iota((27, 256), 0)
    lane = iota((27, 256), 1)
    place = (tap % 3) * 64 + (tap // 3 % 3) * 16 + tap // 9
    base = lax.dot_general(first_ref[...], (place == lane).astype(BF16), (((0,), (0,)), ((), ())),
                           preferred_element_type=F32)
    base = jnp.where(place_ref[0] == 0, base, pltpu.roll(base, 4, 1))
    old = iota((256, 256), 0)
    new = iota((256, 256), 1)
    order = (old % 16 // 8) * 128 + (old // 16 % 4) * 32 + (old // 64) * 8 + old % 8
    permute = (order == new).astype(BF16)
    for x in range(8):
        rows = jnp.concatenate(
            [pltpu.roll(base, x + 16 * b + 64 * e, 1) if x + b + e else base for b in range(2) for e in range(2)], axis=0)
        w1_ref[64 * x:64 * x + 64] = jnp.dot(rows.astype(BF16), permute, preferred_element_type=F32).astype(BF16)

    row = iota((128, 256), 0)
    sz_ref[...] = (iota((128, 256), 1) == (row % 2) * 128 + row // 2 + 4).astype(BF16)
    row = iota((256, 2 * FINE), 0)
    cell = row % 8 + 136 * (row // 128)
    target = (cell % 2) * FINE + (row % 128 // 8) * ROW + cell // 2
    expand_ref[...] = (iota((256, 2 * FINE), 1) == target).astype(BF16)
    for n in range(2):
        flags_ref[n] = jnp.full((8, 128), place_ref[n + 1].astype(F32))

    for side, target in ((0, w2_ref), (1, w8_ref)):
        fine_ref[...] = jnp.zeros_like(fine_ref)
        for t in range(27):
            at = (t // 3 % 3) * 64 + (t % 3) * 16
            fine_ref[16 * (t // 9):16 * (t // 9) + 16, at:at + 16] = kernels_ref[
                16 * t:16 * t + 16, 16 * side:16 * side + 16].astype(F32)
        for u in range(3):
            block = fine_ref[16 * u:16 * u + 16]
            for n in range(4):
                move = (n // 2) * 64 + (n % 2) * 16
                at = 64 * u + 16 * n
                target[at:at + 16] = (pltpu.roll(block, move, 1) if n else block).astype(BF16)

    joint_ref[...] = jnp.zeros_like(joint_ref)
    for t in range(27):
        piece = kernels_ref[432 + 16 * t:448 + 16 * t].astype(F32)
        for side in range(2):
            at = side * 256 + (t // 3 % 3) * 64 + (t % 3) * 16
            joint_ref[16 * (t // 9):16 * (t // 9) + 16, at:at + 16] = piece[:, 16 * side:16 * side + 16]
    for u in range(3):
        block = joint_ref[16 * u:16 * u + 16]
        for n in range(4):
            move = (n // 2) * 64 + (n % 2) * 16
            at = 64 * u + 16 * n
            rows = (pltpu.roll(block, move, 1) if n else block).astype(BF16)
            for side in range(2):
                w7_ref[side, at:at + 16] = rows[:, 256 * side:256 * side + 256]

    same = (iota((432, 768), 0) == iota((432, 768), 1)).astype(BF16)
    block = lax.dot_general(kernels_ref[864:1296], same, (((0,), (0,)), ((), ())), preferred_element_type=F32)
    for p in range(3):
        w4_ref[32 * p:32 * p + 32] = (pltpu.roll(block, 144 * p, 1) if p else block).astype(BF16)
    deeper_base_ref[...] = jnp.zeros_like(deeper_base_ref)
    for t in range(27):
        deeper_base_ref[:, 32 * t:32 * t + 32] = kernels_ref[1296 + 32 * t:1328 + 32 * t].astype(F32)
    block = deeper_base_ref[...]
    for p in range(4):
        w5_ref[32 * p:32 * p + 32] = (pltpu.roll(block, 288 * p, 1) if p else block).astype(BF16)

    w6_ref[...] = kernels_ref[2160:2288]
    spread = (iota((16, 64), 0) == iota((16, 64), 1) % 16).astype(BF16)
    row_weights = jnp.dot(vectors_ref[:, 144:160].astype(BF16), spread, preferred_element_type=F32)
    row = iota((8, 64), 0)
    group = iota((8, 64), 1) // 16
    chosen = (row % 2 == group // 2) & (row // 2 == group % 2)
    w9_ref[...] = jnp.where(chosen, row_weights, 0.0)
    for n in range(5):
        bias_ref[n] = spread_bias(vectors_ref[:, 16 * n:16 * n + 16], 64)
    for n in range(2):
        bias_ref[5 + n] = spread_bias(vectors_ref[:, 80 + 32 * n:112 + 32 * n], 64)


def prepare_weights(place, first, kernels, vectors):
    shapes = [(512, 256), (192, 256), (96, 768), (128, 1792), (2, 192, 256), (192, 256), (128, 256), (128, 32)]
    vmem = pl.BlockSpec(memory_space=pltpu.VMEM)
    return pl.pallas_call(
        weights_kernel,
        out_shape=[jax.ShapeDtypeStruct(s, BF16) for s in shapes]
        + [jax.ShapeDtypeStruct((8, 64), F32), jax.ShapeDtypeStruct((7, 64, 128), F32),
           jax.ShapeDtypeStruct((256, 2 * FINE), BF16), jax.ShapeDtypeStruct((2, 8, 128), F32)],
        in_specs=[pl.BlockSpec(memory_space=pltpu.SMEM)] + [vmem] * 3,
        out_specs=[vmem] * 12,
        scratch_shapes=[pltpu.VMEM((48, 256), F32), pltpu.VMEM((48, 512), F32), pltpu.VMEM((32, 1792), F32)],
        compiler_params=pltpu.CompilerParams(vmem_limit_bytes=24 * 2**20),
        cost_estimate=pl.CostEstimate(flops=10**7, bytes_accessed=2 * 10**6, transcendentals=0),
        name="weights",
    )(place, first, kernels, vectors)


def pick(flag, yes, no):
    rows = yes.shape[0] // 8
    return jnp.where((jnp.concatenate([flag] * rows, axis=0) if rows > 1 else flag) > 0.5, yes, no)


def edges_kernel(flags_ref, low_ref, a_ref, mid_ref, b_ref, high_ref, left_ref, right_ref, cells_ref):
    odd_y = flags_ref[0]
    for x in range(8):
        planes = [
            jnp.concatenate([low_ref[8 * g + x], ref[x], high_ref[8 * g + x]], axis=0).astype(F32)
            for g, ref in enumerate((a_ref, mid_ref, b_ref))
        ]
        cells_ref[32 * x:32 * x + 32] = pick(odd_y, planes[2], planes[0])
        cells_ref[32 * (8 + x):32 * (8 + x) + 32] = planes[1]
        cells_ref[32 * (16 + x):32 * (16 + x) + 32] = pick(odd_y, planes[0], planes[2])
    left = [jnp.zeros((24, 128), F32)] * 2
    right = [jnp.zeros((24, 128), F32)] * 2
    lane = iota((24, 128), 1)
    for y in range(32):
        b, at = y % 2, 8 * (y // 2)
        rows = cells_ref[pl.ds(y, 24, stride=32), :]
        inside = (lane >= at) & (lane < at + 8)
        left[b] = jnp.where(inside, pltpu.roll(rows, at, 1) if at else rows, left[b])
        right[b] = jnp.where(inside, pltpu.roll(rows, (at + 8) % 128, 1) if at < 120 else rows, right[b])
    left_ref[...] = jnp.concatenate(left, axis=0).astype(BF16)
    right_ref[...] = jnp.concatenate(right, axis=0).astype(BF16)


def pack_edges(flags, *pieces):
    vmem = pl.BlockSpec(memory_space=pltpu.VMEM)
    return pl.pallas_call(
        edges_kernel,
        out_shape=[jax.ShapeDtypeStruct((48, 128), BF16)] * 2 + [jax.ShapeDtypeStruct((768, 128), F32)],
        in_specs=[vmem] * 6,
        out_specs=[vmem] * 3,
        compiler_params=pltpu.CompilerParams(vmem_limit_bytes=8 * 2**20),
        name="edges",
    )(flags, *pieces)


def sample_kernel(cells_ref, sz_ref, phase_ref, even_ref, odd_ref):
    for at in range(0, 768, 256):
        sampled = jnp.dot(cells_ref[at:at + 256].astype(BF16), sz_ref[...], preferred_element_type=F32)
        even_ref[at:at + 256] = sampled[:, 0:128]
        odd_ref[at:at + 256] = sampled[:, 128:256]
    for y in range(32):
        to = ROW * (y // 2)
        for e, ref in enumerate((even_ref, odd_ref)):
            phase_ref[2 * (y % 2) + e, :, to:to + ROW] = ref[pl.ds(y, 24, stride=32), :][:, 0:ROW]


def sample(cells, sz):
    vmem = pl.BlockSpec(memory_space=pltpu.VMEM)
    return pl.pallas_call(
        sample_kernel,
        out_shape=jax.ShapeDtypeStruct((4, 24, FINE), F32),
        in_specs=[vmem] * 2,
        out_specs=vmem,
        scratch_shapes=[pltpu.VMEM((768, 128), F32), pltpu.VMEM((768, 128), F32)],
        compiler_params=pltpu.CompilerParams(vmem_limit_bytes=8 * 2**20),
        cost_estimate=pl.CostEstimate(flops=10**8, bytes_accessed=10**6, transcendentals=0),
        name="sample",
    )(cells, sz)


def chunks(width):
    return [slice(at, min(at + 256, width)) for at in range(0, width, 256)]


def moved(values, step):
    return pltpu.roll(values, step % values.shape[1], 1) if step else values


def shifted(values, start, width):
    whole = start // 128 * 128
    if start >= 0 and whole + width + 128 <= values.shape[1]:
        values, start = values[:, whole:whole + width + 128], start - whole
    return moved(values, -start)[:, 0:width]


def window_steps(values, start, width, target_ref):
    for b in range(2):
        even = values[32 * b:32 * b + 16]
        odd = values[32 * b + 16:32 * b + 32]
        rows = jnp.concatenate([moved(odd, 1), even, odd, moved(even, -1)], axis=0)
        at = 64 + 64 * b
        target_ref[at:at + 64] = shifted(rows, start, width)
        yield
        at = 192 - 192 * b
        target_ref[at:at + 64] = shifted(rows, start + ROW - 2 * ROW * b, width)
        yield


def together(*steps):
    steps = list(steps)
    while steps:
        for work in list(steps):
            if next(work, work) is work:
                steps.remove(work)


def neighbours(values, start, width):
    rows = jnp.concatenate([moved(values, 1), values, moved(values, -1)], axis=0)
    return jnp.concatenate([shifted(rows, start + ROW * step, width) for step in (-1, 0, 1)], axis=0)


def two_planes(sums_a, sums_b, acc_ref, part):
    done_a = acc_ref[1, :, part] + sums_a[128:192]
    done_b = acc_ref[0, :, part] + sums_a[64:128] + sums_b[128:192]
    acc_ref[1, :, part] = sums_a[0:64] + sums_b[64:128]
    acc_ref[0, :, part] = sums_b[0:64]
    return done_a, done_b


def paired_dots(w_ref, ref_a, ref_b, width):
    whole = width // 256 * 256
    for at in range(0, whole, 256):
        part = slice(at, at + 256)
        yield part, [jnp.dot(w_ref[...], ref[:, part], preferred_element_type=F32) for ref in (ref_a, ref_b)]
    if whole < width:
        part = slice(whole, width)
        both = jnp.dot(w_ref[...], jnp.concatenate([ref_a[:, part], ref_b[:, part]], axis=1), preferred_element_type=F32)
        yield part, [both[:, 0:width - whole], both[:, width - whole:]]


def wide(bias, values):
    rows, columns = values.shape
    bias = jnp.concatenate([bias] * (columns // 128), axis=1) if columns > 128 else bias
    return jnp.concatenate([bias] * (rows // bias.shape[0]), axis=0) if rows > bias.shape[0] else bias


def network_kernel(flags_ref, center_ref, edge_a_ref, edge_b_ref,
                   w1_ref, w2_ref, w4_ref, w5_ref, w7_ref, w8_ref, w6_ref, w9_ref, bias_ref, expand_ref,
                   out_ref,
                   col0_ref, first_ref, slot_a_ref, slot_b_ref, acc_ref, last_acc_ref,
                   skip_ref, pool_ref, col4_ref, col5_ref, col7_ref, raised_ref, merged_ref, col8_ref, flat_ref, last_ref):
    odd_z = flags_ref[1]
    edge_a = edge_a_ref[...].astype(F32)
    edge_b = edge_b_ref[...].astype(F32)
    edges = jnp.concatenate([pick(odd_z, edge_b, edge_a), pick(odd_z, edge_a, edge_b)], axis=1).astype(BF16)
    placed = [jnp.dot(edges, expand_ref[:, FINE * e:FINE * e + FINE], preferred_element_type=F32) for e in range(2)]
    rows = []
    for b in range(2):
        even, odd = [center_ref[2 * b + e] + placed[e][24 * b:24 * b + 24] for e in range(2)]
        rows.append([moved(odd, 1), even, odd, moved(even, -1)])
    for g in range(3):
        even, odd = [
            jnp.concatenate([part[8 * g:8 * g + 8] for part in rows[b]], axis=0).astype(BF16) for b in range(2)
        ]
        col0_ref[128 * g:128 * g + 128] = jnp.concatenate([moved(odd, ROW), even, odd, moved(even, -ROW)], axis=0)

    bias = bias_ref[0]
    w1_first_ref = w1_ref.at[0:128, 0:128]
    for part, sums in paired_dots(w1_ref, col0_ref.at[0:256], col0_ref.at[128:384], FINE):
        for g in range(2):
            values = leaky(sums[g] + wide(bias, sums[g])).astype(BF16)
            first_ref[8 * g:8 * g + 8, :, part] = values.reshape(8, 64, values.shape[1])
    for part in chunks(FINE):
        sums = jnp.dot(w1_first_ref[...], col0_ref[256:384, part], preferred_element_type=F32)
        values = leaky(sums + wide(bias, sums)).astype(BF16)
        first_ref[16:18, :, part] = values.reshape(2, 64, values.shape[1])

    bias_second = bias_ref[1]

    def gather_first(j, slot_ref):
        for a in range(2):
            yield from window_steps(first_ref[2 * j + a], 0, FINE, slot_ref.at[a])

    def skipped_planes(j, slot_ref):
        for part, sums in paired_dots(w2_ref, slot_ref.at[0], slot_ref.at[1], FINE):
            yield
            top = None
            for a, done in enumerate(two_planes(*sums, acc_ref, part)):
                values = leaky(done + wide(bias_second, done))
                skip_ref[j, 64 * a:64 * a + 64, part] = values.astype(BF16)
                highest = jnp.max(values.reshape(4, 16, values.shape[1]), axis=0)
                top = highest if top is None else jnp.maximum(top, highest)
            pool_ref[j, :, part] = top.astype(BF16)
            yield

    def gather_pool(planes):
        for s in planes:
            col4_ref[144 * s:144 * s + 144] = neighbours(pool_ref[s + 1], COARSE, COARSE_WIDTH)
            yield

    together(gather_first(0, slot_a_ref))

    def two_steps(t, carry):
        together(skipped_planes(2 * t, slot_a_ref), gather_first(2 * t + 1, slot_b_ref))
        together(skipped_planes(2 * t + 1, slot_b_ref), gather_first(2 * t + 2, slot_a_ref))
        return carry

    lax.fori_loop(0, 4, two_steps, 0, unroll=2)
    col4_ref[1152:1200] = jnp.zeros((48, COARSE_WIDTH), BF16)
    col5_ref[1728:1792] = jnp.zeros((64, RAISED_WIDTH), BF16)
    together(skipped_planes(8, slot_a_ref), gather_pool(range(7)))
    together(gather_pool([7]))

    bias_coarse = bias_ref[5, 0:32]
    coarse_parts = [[], []]

    def coarse_planes():
        for _, sums in paired_dots(w4_ref, col4_ref.at[0:768], col4_ref.at[432:1200], COARSE_WIDTH):
            yield
            for m in range(2):
                coarse_parts[m].append(leaky(sums[m] + wide(bias_coarse, sums[m])).astype(BF16))
            yield

    def gather_skipped(planes):
        for d in planes:
            for a in range(2):
                yield from window_steps(skip_ref[d + 3, 64 * a:64 * a + 64], RAISED, RAISED_WIDTH, col7_ref.at[2 * d + a])

    together(coarse_planes(), gather_skipped(range(2)))

    def gather_coarse():
        for m in range(2):
            values = jnp.concatenate(coarse_parts[m], axis=1)
            for p in range(3):
                at = 288 * (3 * m + p)
                col5_ref[at:at + 288] = neighbours(values[32 * p:32 * p + 32], RAISED - COARSE, RAISED_WIDTH)
                yield

    def merged_skipped(pairs):
        for j in pairs:
            for part, sums in paired_dots(w7_ref.at[1], col7_ref.at[2 * j], col7_ref.at[2 * j + 1], RAISED_WIDTH):
                yield
                for a, done in enumerate(two_planes(*sums, acc_ref, part)):
                    if j > 0:
                        merged_ref[2 * j + a - 2, :, part] = done
                yield

    together(gather_coarse(), merged_skipped(range(2)))

    bias_deeper = bias_ref[6, 0:32]
    deeper_parts = []

    def deeper_planes():
        for part in chunks(RAISED_WIDTH):
            sums = jnp.dot(w5_ref[...], col5_ref[:, part], preferred_element_type=F32)
            yield
            deeper_parts.append(leaky(sums + wide(bias_deeper, sums)).astype(BF16))
            yield

    together(deeper_planes(), gather_skipped(range(2, 4)))
    deeper = jnp.concatenate(deeper_parts, axis=1)

    bias_raised = bias_ref[2]
    raised_parts = [[], [], [], []]

    def raised_planes(d):
        for part in chunks(RAISED_WIDTH):
            sums = jnp.dot(w6_ref[...], deeper[32 * d:32 * d + 32, part], preferred_element_type=F32)
            yield
            raised_parts[d].append(leaky(sums + wide(bias_raised, sums)).astype(BF16))
            yield

    def gather_raised(d):
        values = jnp.concatenate(raised_parts[d], axis=1)
        for a in range(2):
            yield from window_steps(values[64 * a:64 * a + 64], 0, RAISED_WIDTH, raised_ref.at[2 * d + a])

    bias_joined = bias_ref[3]
    merged_parts = {}

    def merged_planes(j):
        merged_parts[j] = [[], []]
        for part, sums in paired_dots(w7_ref.at[0], raised_ref.at[2 * j], raised_ref.at[2 * j + 1], RAISED_WIDTH):
            yield
            for a, done in enumerate(two_planes(*sums, acc_ref, part)):
                if j > 0:
                    done = done + merged_ref[2 * j + a - 2, :, part]
                    merged_parts[j][a].append(leaky(done + wide(bias_joined, done)).astype(BF16))
            yield

    def gather_merged(j):
        for a in range(2):
            values = jnp.concatenate(merged_parts[j][a], axis=1)
            yield from window_steps(values, FINAL - RAISED, FINAL_WIDTH, col8_ref.at[2 * j + a - 2])

    bias_final = bias_ref[4]
    output_matrix = w9_ref[...].astype(BF16)

    def final_planes(j):
        for part, sums in paired_dots(w8_ref, col8_ref.at[2 * j], col8_ref.at[2 * j + 1], FINAL_WIDTH):
            yield
            done = two_planes(*sums, last_acc_ref, part)
            if j > 0:
                for a in range(2):
                    values = leaky(done[a] + wide(bias_final, done[a])).astype(BF16)
                    predicted = jnp.dot(output_matrix, values, preferred_element_type=F32)
                    to = 4 * (j - 1) + 2 * a
                    flat_ref[0, to:to + 2, part] = predicted[0:2]
                    flat_ref[1, to:to + 2, part] = predicted[2:4]
            yield

    together(raised_planes(0), merged_skipped([2]))
    together(gather_raised(0), raised_planes(1), merged_skipped([3]))
    together(gather_raised(1), raised_planes(2), merged_planes(0))
    together(gather_raised(2), raised_planes(3), merged_planes(1))
    together(gather_raised(3), merged_planes(2), gather_merged(1))
    together(merged_planes(3), gather_merged(2), final_planes(0))
    together(gather_merged(3), final_planes(1))
    together(final_planes(2))

    for y in range(8):
        at = ROW * (y + 4) - FINAL + 4
        last_ref[8 * y:8 * y + 8, 0:64] = flat_ref[0, :, at:at + 64]
        last_ref[8 * y:8 * y + 8, 64:128] = flat_ref[1, :, at:at + 64]
    old = iota((128, 128), 0)
    turns = (2 * (old % 64) + old // 64 == iota((128, 128), 1)).astype(F32)
    result = jnp.dot(last_ref[...], turns, preferred_element_type=F32, precision=lax.Precision.HIGHEST)
    for y in range(8):
        for x in range(4):
            at = 8 * y + 2 * x
            out_ref[x, 2 * y:2 * y + 2, :] = result[at:at + 2]


def network(flags, center, edge_a, edge_b, weights):
    vmem = pl.BlockSpec(memory_space=pltpu.VMEM)
    scratch = [
        ((384, FINE), BF16), ((18, 64, FINE), BF16), ((2, 256, FINE), BF16), ((2, 256, FINE), BF16),
        ((2, 64, FINE), F32), ((2, 64, FINAL_WIDTH), F32), ((9, 128, FINE), BF16), ((9, 16, FINE), BF16),
        ((1200, COARSE_WIDTH), BF16), ((1792, RAISED_WIDTH), BF16), ((8, 256, RAISED_WIDTH), BF16),
        ((8, 256, RAISED_WIDTH), BF16), ((6, 64, RAISED_WIDTH), F32), ((6, 256, FINAL_WIDTH), BF16),
        ((2, 8, FINAL_WIDTH), F32), ((64, 128), F32),
    ]
    operands = (flags, center, edge_a, edge_b, *weights)
    return pl.pallas_call(
        network_kernel,
        out_shape=jax.ShapeDtypeStruct((4, 16, 128), F32),
        in_specs=[vmem] * len(operands),
        out_specs=vmem,
        scratch_shapes=[pltpu.VMEM(shape, kind) for shape, kind in scratch],
        compiler_params=pltpu.CompilerParams(vmem_limit_bytes=50 * 2**20),
        cost_estimate=pl.CostEstimate(flops=4 * 10**9, bytes_accessed=4 * 10**6, transcendentals=0),
        name="network",
    )(*operands)


def ring(size, step):
    return [(i, (i + step) % size) for i in range(size)]


def partner(i, size, first):
    return (i + 1 if (i % 2 == 1) == first else i - 1) % size


def swaps_y(first):
    return [(gx, 2 * partner(gx // 2, 4, first) + gx % 2) for gx in range(8)]


def swaps_z(first):
    pairs = []
    for gx in range(8):
        for gz in range(8):
            to = partner(gx % 2 * 8 + gz, 16, first)
            pairs.append((gx * 8 + gz, (gx // 2 * 2 + to // 8) * 8 + to % 8))
    return pairs


def exchange(density, half, pack):
    other = lax.ppermute(density, "gx", [(i, i ^ 1) for i in range(8)])
    other, flags = yield other
    mid = jnp.concatenate([jnp.where(half == 0, density, other), jnp.where(half == 0, other, density)], axis=0)
    a = lax.ppermute(mid, "gx", swaps_y(True))
    b = lax.ppermute(mid, "gx", swaps_y(False))
    high = jnp.concatenate([a[:, 8:], mid[:, 8:], b[:, 8:]], axis=0)
    low = jnp.concatenate([a[:, :8], mid[:, :8], b[:, :8]], axis=0)
    low, high = lax.ppermute(high, "gy", ring(8, 1)), lax.ppermute(low, "gy", ring(8, -1))
    left, right, cells = pack(flags, low, a, mid, b, high)
    odd = lax.axis_index("gz") % 2 == 1
    edge_a = lax.ppermute(jnp.where(odd, right, left), ("gx", "gz"), swaps_z(True))
    edge_b = lax.ppermute(jnp.where(odd, left, right), ("gx", "gz"), swaps_z(False))
    yield edge_a, edge_b, cells


def body(density, first_kernel, first_bias, second_kernel, second_bias, coarse_kernel, coarse_bias, deeper_kernel,
         deeper_bias, upward_kernel, upward_bias, joined_kernel, joined_bias, final_kernel, final_bias, output_weight):
    half = (lax.axis_index("gx") % 2).astype(jnp.int32)
    place = jnp.stack([half, lax.axis_index("gx") // 2 % 2, lax.axis_index("gz") % 2]).astype(jnp.int32)
    steps = exchange(density, half, pack_edges)
    other = next(steps)
    kernels = jnp.concatenate([
        jnp.concatenate([second_kernel, final_kernel], axis=4).reshape(432, 32), joined_kernel.reshape(432, 32),
        jnp.swapaxes(coarse_kernel, 3, 4).reshape(432, 32), deeper_kernel.reshape(864, 32), upward_kernel.reshape(128, 32),
    ], axis=0)
    vectors = jnp.concatenate([first_bias, second_bias, upward_bias, joined_bias, final_bias, coarse_bias, deeper_bias,
                               output_weight.astype(F32)]).reshape(1, 160)
    weights = prepare_weights(place, first_kernel.reshape(27, 16), kernels, vectors)
    other, weights = lax.optimization_barrier((other, weights))
    *weights, flags = weights
    sz = weights.pop(6)
    edge_a, edge_b, cells = steps.send((other, flags))
    return network(flags, sample(cells, sz), edge_a, edge_b, weights)


def solution(mesh):
    placed = (P("gx", "gy", "gz"),) + (P(),) * 15
    return jax.shard_map(body, mesh=mesh, in_specs=placed, out_specs=P("gx", "gy", "gz"), check_vma=False)
```

```python
import functools

import jax
import jax.numpy as jnp
from jax import lax
from jax.experimental import pallas as pl
from jax.experimental.pallas import tpu as pltpu
from jax.sharding import PartitionSpec as P

F32 = jnp.float32
BF16 = jnp.bfloat16
ROW = 72
FINE = 1152
COARSE, COARSE_WIDTH = 128, 896
RAISED, RAISED_WIDTH = 200, 768
FINAL, FINAL_WIDTH = 272, 640


def leaky(values):
    return jnp.maximum(values, 0.2 * values)


def iota(shape, dim):
    return lax.broadcasted_iota(jnp.int32, shape, dim)


def spread_bias(bias, rows):
    count = bias.shape[1]
    match = iota((rows, count), 0) % count == iota((rows, count), 1)
    return jnp.broadcast_to(jnp.sum(jnp.where(match, bias, 0.0), axis=1, keepdims=True), (rows, 128))


def weights_kernel(place_ref, first_ref, *refs):
    kernels_ref, vectors_ref = refs[:2]
    (w1_ref, w2_ref, w4_ref, w5_ref, w7_ref, w8_ref, sz_ref, w6_ref, w9_ref, bias_ref, expand_ref, flags_ref) = refs[2:14]
    fine_ref, joint_ref, deeper_base_ref = refs[14:]

    tap = iota((27, 256), 0)
    lane = iota((27, 256), 1)
    place = (tap % 3) * 64 + (tap // 3 % 3) * 16 + tap // 9
    base = lax.dot_general(first_ref[...], (place == lane).astype(BF16), (((0,), (0,)), ((), ())),
                           preferred_element_type=F32)
    base = jnp.where(place_ref[0] == 0, base, pltpu.roll(base, 4, 1))
    old = iota((256, 256), 0)
    new = iota((256, 256), 1)
    order = (old % 16 // 8) * 128 + (old // 16 % 4) * 32 + (old // 64) * 8 + old % 8
    permute = (order == new).astype(BF16)
    for x in range(8):
        rows = jnp.concatenate(
            [pltpu.roll(base, x + 16 * b + 64 * e, 1) if x + b + e else base for b in range(2) for e in range(2)], axis=0)
        w1_ref[64 * x:64 * x + 64] = jnp.dot(rows.astype(BF16), permute, preferred_element_type=F32).astype(BF16)

    row = iota((128, 256), 0)
    sz_ref[...] = (iota((128, 256), 1) == (row % 2) * 128 + row // 2 + 4).astype(BF16)
    row = iota((256, 2 * FINE), 0)
    cell = row % 8 + 136 * (row // 128)
    target = (cell % 2) * FINE + (row % 128 // 8) * ROW + cell // 2
    expand_ref[...] = (iota((256, 2 * FINE), 1) == target).astype(BF16)
    for n in range(2):
        flags_ref[n] = jnp.full((8, 128), place_ref[n + 1].astype(F32))

    for side, target in ((0, w2_ref), (1, w8_ref)):
        fine_ref[...] = jnp.zeros_like(fine_ref)
        for t in range(27):
            at = (t // 3 % 3) * 64 + (t % 3) * 16
            fine_ref[16 * (t // 9):16 * (t // 9) + 16, at:at + 16] = kernels_ref[
                16 * t:16 * t + 16, 16 * side:16 * side + 16].astype(F32)
        for u in range(3):
            block = fine_ref[16 * u:16 * u + 16]
            for n in range(4):
                move = (n // 2) * 64 + (n % 2) * 16
                at = 64 * u + 16 * n
                target[at:at + 16] = (pltpu.roll(block, move, 1) if n else block).astype(BF16)

    joint_ref[...] = jnp.zeros_like(joint_ref)
    for t in range(27):
        piece = kernels_ref[432 + 16 * t:448 + 16 * t].astype(F32)
        for side in range(2):
            at = side * 256 + (t // 3 % 3) * 64 + (t % 3) * 16
            joint_ref[16 * (t // 9):16 * (t // 9) + 16, at:at + 16] = piece[:, 16 * side:16 * side + 16]
    for u in range(3):
        block = joint_ref[16 * u:16 * u + 16]
        for n in range(4):
            move = (n // 2) * 64 + (n % 2) * 16
            at = 64 * u + 16 * n
            rows = (pltpu.roll(block, move, 1) if n else block).astype(BF16)
            for side in range(2):
                w7_ref[side, at:at + 16] = rows[:, 256 * side:256 * side + 256]

    same = (iota((432, 768), 0) == iota((432, 768), 1)).astype(BF16)
    block = lax.dot_general(kernels_ref[864:1296], same, (((0,), (0,)), ((), ())), preferred_element_type=F32)
    for p in range(3):
        w4_ref[32 * p:32 * p + 32] = (pltpu.roll(block, 144 * p, 1) if p else block).astype(BF16)
    deeper_base_ref[...] = jnp.zeros_like(deeper_base_ref)
    for t in range(27):
        deeper_base_ref[:, 32 * t:32 * t + 32] = kernels_ref[1296 + 32 * t:1328 + 32 * t].astype(F32)
    block = deeper_base_ref[...]
    for p in range(4):
        w5_ref[32 * p:32 * p + 32] = (pltpu.roll(block, 288 * p, 1) if p else block).astype(BF16)

    w6_ref[...] = kernels_ref[2160:2288]
    spread = (iota((16, 64), 0) == iota((16, 64), 1) % 16).astype(BF16)
    row_weights = jnp.dot(vectors_ref[:, 144:160].astype(BF16), spread, preferred_element_type=F32)
    row = iota((8, 64), 0)
    group = iota((8, 64), 1) // 16
    chosen = (row % 2 == group // 2) & (row // 2 == group % 2)
    w9_ref[...] = jnp.where(chosen, row_weights, 0.0)
    for n in range(5):
        bias_ref[n] = spread_bias(vectors_ref[:, 16 * n:16 * n + 16], 64)
    for n in range(2):
        bias_ref[5 + n] = spread_bias(vectors_ref[:, 80 + 32 * n:112 + 32 * n], 64)


def prepare_weights(place, first, kernels, vectors):
    shapes = [(512, 256), (192, 256), (96, 768), (128, 1792), (2, 192, 256), (192, 256), (128, 256), (128, 32)]
    vmem = pl.BlockSpec(memory_space=pltpu.VMEM)
    return pl.pallas_call(
        weights_kernel,
        out_shape=[jax.ShapeDtypeStruct(s, BF16) for s in shapes]
        + [jax.ShapeDtypeStruct((8, 64), F32), jax.ShapeDtypeStruct((7, 64, 128), F32),
           jax.ShapeDtypeStruct((256, 2 * FINE), BF16), jax.ShapeDtypeStruct((2, 8, 128), F32)],
        in_specs=[pl.BlockSpec(memory_space=pltpu.SMEM)] + [vmem] * 3,
        out_specs=[vmem] * 12,
        scratch_shapes=[pltpu.VMEM((48, 256), F32), pltpu.VMEM((48, 512), F32), pltpu.VMEM((32, 1792), F32)],
        compiler_params=pltpu.CompilerParams(vmem_limit_bytes=24 * 2**20),
        cost_estimate=pl.CostEstimate(flops=10**7, bytes_accessed=2 * 10**6, transcendentals=0),
        name="weights",
    )(place, first, kernels, vectors)


def pick(flag, yes, no):
    rows = yes.shape[0] // 8
    return jnp.where((jnp.concatenate([flag] * rows, axis=0) if rows > 1 else flag) > 0.5, yes, no)


def edges_kernel(flags_ref, low_ref, a_ref, mid_ref, b_ref, high_ref, left_ref, right_ref, cells_ref):
    odd_y = flags_ref[0]
    for x in range(8):
        planes = [
            jnp.concatenate([low_ref[8 * g + x], ref[x], high_ref[8 * g + x]], axis=0).astype(F32)
            for g, ref in enumerate((a_ref, mid_ref, b_ref))
        ]
        cells_ref[32 * x:32 * x + 32] = pick(odd_y, planes[2], planes[0])
        cells_ref[32 * (8 + x):32 * (8 + x) + 32] = planes[1]
        cells_ref[32 * (16 + x):32 * (16 + x) + 32] = pick(odd_y, planes[0], planes[2])
    left = [jnp.zeros((24, 128), F32)] * 2
    right = [jnp.zeros((24, 128), F32)] * 2
    lane = iota((24, 128), 1)
    for y in range(32):
        b, at = y % 2, 8 * (y // 2)
        rows = cells_ref[pl.ds(y, 24, stride=32), :]
        inside = (lane >= at) & (lane < at + 8)
        left[b] = jnp.where(inside, pltpu.roll(rows, at, 1) if at else rows, left[b])
        right[b] = jnp.where(inside, pltpu.roll(rows, (at + 8) % 128, 1) if at < 120 else rows, right[b])
    left_ref[...] = jnp.concatenate(left, axis=0).astype(BF16)
    right_ref[...] = jnp.concatenate(right, axis=0).astype(BF16)


def pack_edges(flags, *pieces):
    vmem = pl.BlockSpec(memory_space=pltpu.VMEM)
    return pl.pallas_call(
        edges_kernel,
        out_shape=[jax.ShapeDtypeStruct((48, 128), BF16)] * 2 + [jax.ShapeDtypeStruct((768, 128), F32)],
        in_specs=[vmem] * 6,
        out_specs=[vmem] * 3,
        compiler_params=pltpu.CompilerParams(vmem_limit_bytes=8 * 2**20),
        name="edges",
    )(flags, *pieces)


def sample_kernel(cells_ref, sz_ref, phase_ref, even_ref, odd_ref):
    for at in range(0, 768, 256):
        sampled = jnp.dot(cells_ref[at:at + 256].astype(BF16), sz_ref[...], preferred_element_type=F32)
        even_ref[at:at + 256] = sampled[:, 0:128]
        odd_ref[at:at + 256] = sampled[:, 128:256]
    for y in range(32):
        to = ROW * (y // 2)
        for e, ref in enumerate((even_ref, odd_ref)):
            phase_ref[2 * (y % 2) + e, :, to:to + ROW] = ref[pl.ds(y, 24, stride=32), :][:, 0:ROW]


def sample(cells, sz):
    vmem = pl.BlockSpec(memory_space=pltpu.VMEM)
    return pl.pallas_call(
        sample_kernel,
        out_shape=jax.ShapeDtypeStruct((4, 24, FINE), F32),
        in_specs=[vmem] * 2,
        out_specs=vmem,
        scratch_shapes=[pltpu.VMEM((768, 128), F32), pltpu.VMEM((768, 128), F32)],
        compiler_params=pltpu.CompilerParams(vmem_limit_bytes=8 * 2**20),
        cost_estimate=pl.CostEstimate(flops=10**8, bytes_accessed=10**6, transcendentals=0),
        name="sample",
    )(cells, sz)


def chunks(width):
    return [slice(at, min(at + 256, width)) for at in range(0, width, 256)]


def moved(values, step):
    return pltpu.roll(values, step % values.shape[1], 1) if step else values


def shifted(values, start, width):
    whole = start // 128 * 128
    if start >= 0 and whole + width + 128 <= values.shape[1]:
        values, start = values[:, whole:whole + width + 128], start - whole
    return moved(values, -start)[:, 0:width]


def window_steps(values, start, width, target_ref):
    for b in range(2):
        even = values[32 * b:32 * b + 16]
        odd = values[32 * b + 16:32 * b + 32]
        rows = jnp.concatenate([moved(odd, 1), even, odd, moved(even, -1)], axis=0)
        at = 64 + 64 * b
        target_ref[at:at + 64] = shifted(rows, start, width)
        yield
        at = 192 - 192 * b
        target_ref[at:at + 64] = shifted(rows, start + ROW - 2 * ROW * b, width)
        yield


def together(*steps):
    steps = list(steps)
    while steps:
        for work in list(steps):
            if next(work, work) is work:
                steps.remove(work)


def neighbours(values, start, width):
    rows = jnp.concatenate([moved(values, 1), values, moved(values, -1)], axis=0)
    return jnp.concatenate([shifted(rows, start + ROW * step, width) for step in (-1, 0, 1)], axis=0)


def two_planes(sums_a, sums_b, acc_ref, part):
    done_a = acc_ref[1, :, part] + sums_a[128:192]
    done_b = acc_ref[0, :, part] + sums_a[64:128] + sums_b[128:192]
    acc_ref[1, :, part] = sums_a[0:64] + sums_b[64:128]
    acc_ref[0, :, part] = sums_b[0:64]
    return done_a, done_b


def paired_dots(w_ref, ref_a, ref_b, width):
    whole = width // 256 * 256
    for at in range(0, whole, 256):
        part = slice(at, at + 256)
        yield part, [jnp.dot(w_ref[...], ref[:, part], preferred_element_type=F32) for ref in (ref_a, ref_b)]
    if whole < width:
        part = slice(whole, width)
        both = jnp.dot(w_ref[...], jnp.concatenate([ref_a[:, part], ref_b[:, part]], axis=1), preferred_element_type=F32)
        yield part, [both[:, 0:width - whole], both[:, width - whole:]]


def wide(bias, values):
    rows, columns = values.shape
    bias = jnp.concatenate([bias] * (columns // 128), axis=1) if columns > 128 else bias
    return jnp.concatenate([bias] * (rows // bias.shape[0]), axis=0) if rows > bias.shape[0] else bias


def network_kernel(flags_ref, center_ref, edge_a_ref, edge_b_ref,
                   w1_ref, w2_ref, w4_ref, w5_ref, w7_ref, w8_ref, w6_ref, w9_ref, bias_ref, expand_ref,
                   out_ref,
                   col0_ref, first_ref, slot_a_ref, slot_b_ref, acc_ref, last_acc_ref,
                   skip_ref, pool_ref, col4_ref, col5_ref, col7_ref, raised_ref, merged_ref, col8_ref, flat_ref, last_ref):
    odd_z = flags_ref[1]
    edge_a = edge_a_ref[...].astype(F32)
    edge_b = edge_b_ref[...].astype(F32)
    edges = jnp.concatenate([pick(odd_z, edge_b, edge_a), pick(odd_z, edge_a, edge_b)], axis=1).astype(BF16)
    placed = [jnp.dot(edges, expand_ref[:, FINE * e:FINE * e + FINE], preferred_element_type=F32) for e in range(2)]
    rows = []
    for b in range(2):
        even, odd = [center_ref[2 * b + e] + placed[e][24 * b:24 * b + 24] for e in range(2)]
        rows.append([moved(odd, 1), even, odd, moved(even, -1)])
    for g in range(3):
        even, odd = [
            jnp.concatenate([part[8 * g:8 * g + 8] for part in rows[b]], axis=0).astype(BF16) for b in range(2)
        ]
        col0_ref[128 * g:128 * g + 128] = jnp.concatenate([moved(odd, ROW), even, odd, moved(even, -ROW)], axis=0)

    bias = bias_ref[0]
    w1_first_ref = w1_ref.at[0:128, 0:128]
    for part, sums in paired_dots(w1_ref, col0_ref.at[0:256], col0_ref.at[128:384], FINE):
        for g in range(2):
            values = leaky(sums[g] + wide(bias, sums[g])).astype(BF16)
            first_ref[8 * g:8 * g + 8, :, part] = values.reshape(8, 64, values.shape[1])
    for part in chunks(FINE):
        sums = jnp.dot(w1_first_ref[...], col0_ref[256:384, part], preferred_element_type=F32)
        values = leaky(sums + wide(bias, sums)).astype(BF16)
        first_ref[16:18, :, part] = values.reshape(2, 64, values.shape[1])

    bias_second = bias_ref[1]

    def gather_first(j, slot_ref):
        for a in range(2):
            yield from window_steps(first_ref[2 * j + a], 0, FINE, slot_ref.at[a])

    def skipped_planes(j, slot_ref):
        for part, sums in paired_dots(w2_ref, slot_ref.at[0], slot_ref.at[1], FINE):
            yield
            top = None
            for a, done in enumerate(two_planes(*sums, acc_ref, part)):
                values = leaky(done + wide(bias_second, done))
                skip_ref[j, 64 * a:64 * a + 64, part] = values.astype(BF16)
                highest = jnp.max(values.reshape(4, 16, values.shape[1]), axis=0)
                top = highest if top is None else jnp.maximum(top, highest)
            pool_ref[j, :, part] = top.astype(BF16)
            yield

    def gather_pool(planes):
        for s in planes:
            col4_ref[144 * s:144 * s + 144] = neighbours(pool_ref[s + 1], COARSE, COARSE_WIDTH)
            yield

    together(gather_first(0, slot_a_ref))

    def two_steps(t, carry):
        together(skipped_planes(2 * t, slot_a_ref), gather_first(2 * t + 1, slot_b_ref))
        together(skipped_planes(2 * t + 1, slot_b_ref), gather_first(2 * t + 2, slot_a_ref))
        return carry

    lax.fori_loop(0, 4, two_steps, 0, unroll=4)
    col4_ref[1152:1200] = jnp.zeros((48, COARSE_WIDTH), BF16)
    col5_ref[1728:1792] = jnp.zeros((64, RAISED_WIDTH), BF16)
    together(skipped_planes(8, slot_a_ref), gather_pool(range(7)))
    together(gather_pool([7]))

    bias_coarse = bias_ref[5, 0:32]
    coarse_parts = [[], []]

    def coarse_planes():
        for _, sums in paired_dots(w4_ref, col4_ref.at[0:768], col4_ref.at[432:1200], COARSE_WIDTH):
            yield
            for m in range(2):
                coarse_parts[m].append(leaky(sums[m] + wide(bias_coarse, sums[m])).astype(BF16))
            yield

    def gather_skipped(planes):
        for d in planes:
            for a in range(2):
                yield from window_steps(skip_ref[d + 3, 64 * a:64 * a + 64], RAISED, RAISED_WIDTH, col7_ref.at[2 * d + a])

    together(coarse_planes(), gather_skipped(range(2)))

    def gather_coarse():
        for m in range(2):
            values = jnp.concatenate(coarse_parts[m], axis=1)
            for p in range(3):
                at = 288 * (3 * m + p)
                col5_ref[at:at + 288] = neighbours(values[32 * p:32 * p + 32], RAISED - COARSE, RAISED_WIDTH)
                yield

    def merged_skipped(pairs):
        for j in pairs:
            for part, sums in paired_dots(w7_ref.at[1], col7_ref.at[2 * j], col7_ref.at[2 * j + 1], RAISED_WIDTH):
                yield
                for a, done in enumerate(two_planes(*sums, acc_ref, part)):
                    if j > 0:
                        merged_ref[2 * j + a - 2, :, part] = done
                yield

    together(gather_coarse(), merged_skipped(range(2)))

    bias_deeper = bias_ref[6, 0:32]
    deeper_parts = []

    def deeper_planes():
        for part in chunks(RAISED_WIDTH):
            sums = jnp.dot(w5_ref[...], col5_ref[:, part], preferred_element_type=F32)
            yield
            deeper_parts.append(leaky(sums + wide(bias_deeper, sums)).astype(BF16))
            yield

    together(deeper_planes(), gather_skipped(range(2, 4)))
    deeper = jnp.concatenate(deeper_parts, axis=1)

    bias_raised = bias_ref[2]
    raised_parts = [[], [], [], []]

    def raised_planes(d):
        for part in chunks(RAISED_WIDTH):
            sums = jnp.dot(w6_ref[...], deeper[32 * d:32 * d + 32, part], preferred_element_type=F32)
            yield
            raised_parts[d].append(leaky(sums + wide(bias_raised, sums)).astype(BF16))
            yield

    def gather_raised(d):
        values = jnp.concatenate(raised_parts[d], axis=1)
        for a in range(2):
            yield from window_steps(values[64 * a:64 * a + 64], 0, RAISED_WIDTH, raised_ref.at[2 * d + a])

    bias_joined = bias_ref[3]
    merged_parts = {}

    def merged_planes(j):
        merged_parts[j] = [[], []]
        for part, sums in paired_dots(w7_ref.at[0], raised_ref.at[2 * j], raised_ref.at[2 * j + 1], RAISED_WIDTH):
            yield
            for a, done in enumerate(two_planes(*sums, acc_ref, part)):
                if j > 0:
                    done = done + merged_ref[2 * j + a - 2, :, part]
                    merged_parts[j][a].append(leaky(done + wide(bias_joined, done)).astype(BF16))
            yield

    def gather_merged(j):
        for a in range(2):
            values = jnp.concatenate(merged_parts[j][a], axis=1)
            yield from window_steps(values, FINAL - RAISED, FINAL_WIDTH, col8_ref.at[2 * j + a - 2])

    bias_final = bias_ref[4]
    output_matrix = w9_ref[...].astype(BF16)

    def final_planes(j):
        for part, sums in paired_dots(w8_ref, col8_ref.at[2 * j], col8_ref.at[2 * j + 1], FINAL_WIDTH):
            yield
            done = two_planes(*sums, last_acc_ref, part)
            if j > 0:
                for a in range(2):
                    values = leaky(done[a] + wide(bias_final, done[a])).astype(BF16)
                    predicted = jnp.dot(output_matrix, values, preferred_element_type=F32)
                    to = 4 * (j - 1) + 2 * a
                    flat_ref[0, to:to + 2, part] = predicted[0:2]
                    flat_ref[1, to:to + 2, part] = predicted[2:4]
            yield

    together(raised_planes(0), merged_skipped([2]))
    together(gather_raised(0), raised_planes(1), merged_skipped([3]))
    together(gather_raised(1), raised_planes(2), merged_planes(0))
    together(gather_raised(2), raised_planes(3), merged_planes(1))
    together(gather_raised(3), merged_planes(2), gather_merged(1))
    together(merged_planes(3), gather_merged(2), final_planes(0))
    together(gather_merged(3), final_planes(1))
    together(final_planes(2))

    for y in range(8):
        at = ROW * (y + 4) - FINAL + 4
        last_ref[8 * y:8 * y + 8, 0:64] = flat_ref[0, :, at:at + 64]
        last_ref[8 * y:8 * y + 8, 64:128] = flat_ref[1, :, at:at + 64]
    old = iota((128, 128), 0)
    turns = (2 * (old % 64) + old // 64 == iota((128, 128), 1)).astype(F32)
    result = jnp.dot(last_ref[...], turns, preferred_element_type=F32, precision=lax.Precision.HIGHEST)
    for y in range(8):
        for x in range(4):
            at = 8 * y + 2 * x
            out_ref[x, 2 * y:2 * y + 2, :] = result[at:at + 2]


def network(flags, center, edge_a, edge_b, weights):
    vmem = pl.BlockSpec(memory_space=pltpu.VMEM)
    scratch = [
        ((384, FINE), BF16), ((18, 64, FINE), BF16), ((2, 256, FINE), BF16), ((2, 256, FINE), BF16),
        ((2, 64, FINE), F32), ((2, 64, FINAL_WIDTH), F32), ((9, 128, FINE), BF16), ((9, 16, FINE), BF16),
        ((1200, COARSE_WIDTH), BF16), ((1792, RAISED_WIDTH), BF16), ((8, 256, RAISED_WIDTH), BF16),
        ((8, 256, RAISED_WIDTH), BF16), ((6, 64, RAISED_WIDTH), F32), ((6, 256, FINAL_WIDTH), BF16),
        ((2, 8, FINAL_WIDTH), F32), ((64, 128), F32),
    ]
    operands = (flags, center, edge_a, edge_b, *weights)
    return pl.pallas_call(
        network_kernel,
        out_shape=jax.ShapeDtypeStruct((4, 16, 128), F32),
        in_specs=[vmem] * len(operands),
        out_specs=vmem,
        scratch_shapes=[pltpu.VMEM(shape, kind) for shape, kind in scratch],
        compiler_params=pltpu.CompilerParams(vmem_limit_bytes=50 * 2**20),
        cost_estimate=pl.CostEstimate(flops=4 * 10**9, bytes_accessed=4 * 10**6, transcendentals=0),
        name="network",
    )(*operands)


def ring(size, step):
    return [(i, (i + step) % size) for i in range(size)]


def partner(i, size, first):
    return (i + 1 if (i % 2 == 1) == first else i - 1) % size


def swaps_y(first):
    return [(gx, 2 * partner(gx // 2, 4, first) + gx % 2) for gx in range(8)]


def swaps_z(first):
    pairs = []
    for gx in range(8):
        for gz in range(8):
            to = partner(gx % 2 * 8 + gz, 16, first)
            pairs.append((gx * 8 + gz, (gx // 2 * 2 + to // 8) * 8 + to % 8))
    return pairs


def exchange(density, half, pack):
    other = lax.ppermute(density, "gx", [(i, i ^ 1) for i in range(8)])
    other, flags = yield other
    mid = jnp.concatenate([jnp.where(half == 0, density, other), jnp.where(half == 0, other, density)], axis=0)
    a = lax.ppermute(mid, "gx", swaps_y(True))
    b = lax.ppermute(mid, "gx", swaps_y(False))
    high = jnp.concatenate([a[:, 8:], mid[:, 8:], b[:, 8:]], axis=0)
    low = jnp.concatenate([a[:, :8], mid[:, :8], b[:, :8]], axis=0)
    low, high = lax.ppermute(high, "gy", ring(8, 1)), lax.ppermute(low, "gy", ring(8, -1))
    left, right, cells = pack(flags, low, a, mid, b, high)
    odd = lax.axis_index("gz") % 2 == 1
    edge_a = lax.ppermute(jnp.where(odd, right, left), ("gx", "gz"), swaps_z(True))
    edge_b = lax.ppermute(jnp.where(odd, left, right), ("gx", "gz"), swaps_z(False))
    yield edge_a, edge_b, cells


def body(density, first_kernel, first_bias, second_kernel, second_bias, coarse_kernel, coarse_bias, deeper_kernel,
         deeper_bias, upward_kernel, upward_bias, joined_kernel, joined_bias, final_kernel, final_bias, output_weight):
    half = (lax.axis_index("gx") % 2).astype(jnp.int32)
    place = jnp.stack([half, lax.axis_index("gx") // 2 % 2, lax.axis_index("gz") % 2]).astype(jnp.int32)
    steps = exchange(density, half, pack_edges)
    other = next(steps)
    kernels = jnp.concatenate([
        jnp.concatenate([second_kernel, final_kernel], axis=4).reshape(432, 32), joined_kernel.reshape(432, 32),
        jnp.swapaxes(coarse_kernel, 3, 4).reshape(432, 32), deeper_kernel.reshape(864, 32), upward_kernel.reshape(128, 32),
    ], axis=0)
    vectors = jnp.concatenate([first_bias, second_bias, upward_bias, joined_bias, final_bias, coarse_bias, deeper_bias,
                               output_weight.astype(F32)]).reshape(1, 160)
    weights = prepare_weights(place, first_kernel.reshape(27, 16), kernels, vectors)
    other, weights = lax.optimization_barrier((other, weights))
    *weights, flags = weights
    sz = weights.pop(6)
    edge_a, edge_b, cells = steps.send((other, flags))
    return network(flags, sample(cells, sz), edge_a, edge_b, weights)


def solution(mesh):
    placed = (P("gx", "gy", "gz"),) + (P(),) * 15
    return jax.shard_map(body, mesh=mesh, in_specs=placed, out_specs=P("gx", "gy", "gz"), check_vma=False)
```
